128 devices in a mesh: seq: 64 (over y, z_hi, x, core), rep: 2 (over z_lo).
Axes of the slice: x: 4, y: 4, z: 4 (z_hi: 2, z_lo: 2; z = z_hi * 2 + z_lo), core: 2. Of those that a mesh axis runs over, the one named last changes fastest.
Arguments:
- layer_input: bfloat16 [2, 256, 256, 1024], P('rep', 'seq'), may hold values from -16 to 16
- out_grad: bfloat16 [2, 256, 256, 1024], P('rep', 'seq'), may hold values from -16 to 16
- slot_frame: int32 [2, 256], P('rep'), may hold values from 0 to 255, each once within a row
- ln_gain: float32 [1024], replicated, may hold values from 0.5 to 1.5
- ln_bias: float32 [1024], replicated, may hold values from -3 to 3
- w_qkv: bfloat16 [1024, 3072], replicated, may hold values from -0.1875 to 0.1875
- w_out: bfloat16 [1024, 1024], replicated, may hold values from -0.1875 to 0.1875
- time_bias: float32 [16, 511], replicated, may hold values from -4 to 240
Outputs:
- in_grad: bfloat16 [2, 256, 256, 1024], P('rep', 'seq')
- qkv_grad: float32 [1024, 3072], P(('seq', 'rep'))
- proj_grad: float32 [1024, 1024], P(('seq', 'rep'))
- gain_grad: float32 [1024], P(('seq', 'rep'))
- bias_grad: float32 [1024], P(('seq', 'rep'))
The draws below stay inside these ranges and needn't reach their ends.
Inputs may be any that keep to these rules, and one draw needn't show every extreme that they name: For each video, slot_frame is a permutation of the frames 0 to 255.
All inputs are finite; a program needn't handle non-finite values.
Results may differ from the reference program's by a relative error of at most 0.0094.
Values may be sent and summed in bfloat16 or wider, within the bound.
No kernel may reach another device: no remote copies, remote signals or barrier semaphores. Data moves between devices by JAX's collectives and lax.ppermute only.
A program may use at most 192 MiB of HBM per device.

```python
import math
import jax
import jax.numpy as jnp
from jax import lax

D = 1024
HEADS = 16
PATCHES = 256
VIDEOS = 2
FRAMES = 256


def draw_time_bias(key, part):
    key = jax.random.fold_in(key, 11)
    base_bias = jnp.clip(jax.random.normal(key, (HEADS, 2 * FRAMES - 1), jnp.float32), -4.0, 4.0)
    return base_bias


def spiked(drawn, own_key, source, target, parts, factor):
    owner, partner = [(jnp.arange(drawn.shape[dim]) // (drawn.shape[dim] // parts)).reshape([-1 if axis == dim else 1 for axis in range(drawn.ndim)]) for dim in (source, target)]
    chosen = jax.random.permutation(own_key, parts)[partner]
    strong = (owner == chosen) | (owner == (partner + parts // 2) % parts)
    return jnp.where(strong, factor * drawn, drawn)


def levels(own_key, extent, cuts, smallest, high):
    level = 1.0
    for dim, parts in cuts:
        heights = jax.random.uniform(jax.random.fold_in(jax.random.fold_in(own_key, 6), dim), (parts,), jnp.float32, smallest / len(cuts), high / len(cuts))
        level = level * jnp.repeat(jnp.exp(heights), extent[dim] // parts).reshape((-1,) + (1,) * (len(extent) - 1 - dim))
    return level


def gaussian(own_key, dims, width, limit, split=(), held_as=jnp.bfloat16):
    values = jax.random.normal(own_key, dims, jnp.float32) * width
    if len(split) > 0:
        values = levels(own_key, dims, split, -0.22, 0.18) * values
    return jnp.clip(values, min=-limit, max=limit).astype(held_as)


def heavy_noise(stream_key, extent, spread, most, cuts, heavy, kind=jnp.bfloat16):
    entries = spread * jax.random.normal(stream_key, extent, jnp.float32)
    if cuts:
        entries = entries * levels(stream_key, extent, cuts, -0.22, 0.18)
    return jnp.clip(spiked(entries, jax.random.fold_in(stream_key, 3), *heavy), -most, most).astype(kind)


def setup_inputs(seed: int = 0) -> dict:
    key_list = jax.random.split(jax.random.key(seed), 9)
    layer_input = heavy_noise(key_list[0], (VIDEOS, FRAMES, PATCHES, D), 1.0, 16.0, ((0, 2), (1, 64)), (1, 3, 64, 4.0))
    out_grad = heavy_noise(key_list[1], (VIDEOS, FRAMES, PATCHES, D), 1.0, 16.0, ((0, 2), (1, 64)), (1, 3, 64, 4.0))
    slot_frame = jax.vmap(lambda own: jax.random.permutation(own, FRAMES))(jax.random.split(key_list[2], VIDEOS)).reshape((VIDEOS, FRAMES)).astype(jnp.int32)
    ln_gain = jnp.clip(1.0 + 0.1 * jax.random.normal(key_list[3], (D,), jnp.float32), 0.5, 1.5)
    ln_bias = gaussian(key_list[4], (D,), 0.5, 3.0, (), jnp.float32)
    w_qkv = gaussian(key_list[5], (D, 3 * D), D ** -0.5, 0.1875)
    w_out = gaussian(key_list[6], (D, D), D ** -0.5, 0.1875)
    time_bias = draw_time_bias(jax.random.fold_in(key_list[8], 71), 0)
    return {"layer_input": layer_input, "out_grad": out_grad, "slot_frame": slot_frame, "ln_gain": ln_gain, "ln_bias": ln_bias, "w_qkv": w_qkv, "w_out": w_out, "time_bias": time_bias}


def widen(array):
    return array.astype(jnp.float32)

def expand_bias(time_bias, frames):
    offsets = (jnp.arange(frames, dtype=jnp.int32)[None, :] - jnp.arange(frames, dtype=jnp.int32)[:, None] + frames - 1).astype(jnp.int32)
    return jnp.take(time_bias, offsets, axis=1)

def position_backward(rows_in, rows_grad, ln_gain, ln_bias, w_qkv, w_out, bias_table):
    frames, positions, model_width = rows_in.shape
    head_count = bias_table.shape[0]
    head_dim = model_width // head_count
    factor = head_dim ** (-0.5)
    values_in = widen(rows_in)
    row_mean = lax.optimization_barrier(jnp.mean(values_in, axis=-1, keepdims=True))
    centred = values_in - row_mean
    inv_std = lax.rsqrt(lax.optimization_barrier(jnp.mean(centred * centred, axis=-1, keepdims=True)) + 1e-05)
    normed = centred * inv_std
    hidden = (normed * ln_gain + ln_bias).astype(jnp.bfloat16)
    flat_hidden = hidden.reshape(frames * positions, model_width)
    projected = jnp.dot(flat_hidden, w_qkv, preferred_element_type=jnp.float32).astype(jnp.bfloat16)
    projected = projected.reshape(frames, positions, 3, head_count, head_dim)
    queries = projected[:, :, 0]
    key_rows = projected[:, :, 1]
    val_rows = projected[:, :, 2]
    scores = jnp.einsum('tphe,sphe->phts', widen(queries), widen(key_rows)) * factor + bias_table[None]
    weights = jax.nn.softmax(scores, axis=-1)
    short_weights = weights.astype(jnp.bfloat16)
    attended = jnp.einsum('phts,sphe->tphe', widen(short_weights), widen(val_rows)).astype(jnp.bfloat16)
    attended = attended.reshape(frames * positions, model_width)
    flat_grad = rows_grad.reshape(frames * positions, model_width)
    att_grad = jnp.dot(flat_grad, w_out.T, preferred_element_type=jnp.float32).astype(jnp.bfloat16)
    att_grad = att_grad.reshape(frames, positions, head_count, head_dim)
    proj_term = jnp.dot(flat_grad.T, attended, preferred_element_type=jnp.float32)
    weight_grad = jnp.einsum('tphe,sphe->phts', widen(att_grad), widen(val_rows))
    value_grad = jnp.einsum('phts,tphe->sphe', widen(short_weights), widen(att_grad)).astype(jnp.bfloat16)
    score_grad = (weights * (weight_grad - lax.optimization_barrier(jnp.sum(weight_grad * weights, axis=-1, keepdims=True))) * factor).astype(jnp.bfloat16)
    query_grad = jnp.einsum('phts,sphe->tphe', widen(score_grad), widen(key_rows)).astype(jnp.bfloat16)
    key_grad = jnp.einsum('phts,tphe->sphe', widen(score_grad), widen(queries)).astype(jnp.bfloat16)
    packed = jnp.stack([query_grad, key_grad, value_grad], axis=2).reshape(frames * positions, 3 * model_width)
    qkv_term = jnp.dot(flat_hidden.T, packed, preferred_element_type=jnp.float32)
    hidden_grad = jnp.dot(packed, w_qkv.T, preferred_element_type=jnp.float32).reshape(frames, positions, model_width)
    gain_term = lax.optimization_barrier(jnp.sum(hidden_grad * normed, axis=(0, 1)))
    bias_term = lax.optimization_barrier(jnp.sum(hidden_grad, axis=(0, 1)))
    scaled = hidden_grad * ln_gain
    norm_grad = inv_std * (scaled - lax.optimization_barrier(jnp.mean(scaled, axis=-1, keepdims=True)) - normed * lax.optimization_barrier(jnp.mean(scaled * normed, axis=-1, keepdims=True)))
    result = (widen(rows_grad) + norm_grad).astype(jnp.bfloat16)
    return (result, qkv_term, proj_term, gain_term, bias_term)

def reference(layer_input, out_grad, slot_frame, ln_gain, ln_bias, w_qkv, w_out, time_bias):
    videos, frames, patches, model_width = layer_input.shape
    bias_table = expand_bias(time_bias, frames)
    frame_order = jnp.arange(frames, dtype=jnp.int32)

    def invert(slot_row):
        return jnp.zeros((frames,), jnp.int32).at[slot_row.astype(jnp.int32)].set(frame_order)
    inverse = jax.vmap(invert)(slot_frame)
    natural = jnp.take_along_axis(out_grad, inverse[:, :, None, None], axis=1)
    block_size = math.gcd(patches, 8)
    groups = patches // block_size

    def to_blocks(array):
        shaped = array.reshape(videos, frames, groups, block_size, model_width)
        return shaped.transpose(0, 2, 1, 3, 4).reshape(videos * groups, frames, block_size, model_width)
    zero_sums = (jnp.zeros((model_width, 3 * model_width), jnp.float32), jnp.zeros((model_width, model_width), jnp.float32), jnp.zeros((model_width,), jnp.float32), jnp.zeros((model_width,), jnp.float32))

    def advance(running, inputs_pair):
        outcome = position_backward(inputs_pair[0], inputs_pair[1], ln_gain, ln_bias, w_qkv, w_out, bias_table)
        updated = tuple((total + term for total, term in zip(running, outcome[1:])))
        return (updated, outcome[0])
    totals, results = lax.scan(advance, zero_sums, (to_blocks(layer_input), to_blocks(natural)))
    in_grad = results.reshape(videos, groups, frames, block_size, model_width).transpose(0, 2, 1, 3, 4).reshape(videos, frames, patches, model_width)
    factor = (videos * frames * patches) ** (-0.5)
    return (in_grad, totals[0] * factor, totals[1] * factor, totals[2] * factor, totals[3] * factor)
```

```python
import functools

import jax
import jax.numpy as jnp
from jax import lax
from jax.experimental import pallas as pl
from jax.experimental.pallas import tpu as pltpu
from jax.sharding import Mesh, PartitionSpec as P

BF = jnp.bfloat16
F32 = jnp.float32
VMEM_BYTES = 60 * 1024 * 1024
SPAN = 4
GROUP = 16
PAIR = 128
SEQ = ("y", "zh", "x", "core")
CHIPS = ("y", "zh", "x", "zl")

NT = (((1,), (1,)), ((), ()))
TN = (((0,), (0,)), ((), ()))


def mm(a, b, dims=(((1,), (0,)), ((), ()))):
    return lax.dot_general(a, b, dims, preferred_element_type=F32)


def params(*semantics):
    return pltpu.CompilerParams(vmem_limit_bytes=VMEM_BYTES)


def cost(flops, moved, transcendentals=0):
    return pl.CostEstimate(flops=flops, bytes_accessed=moved, transcendentals=transcendentals)


def full(shape):
    return pl.BlockSpec(shape, lambda *ids: (0,) * len(shape))


def digits(index, *sizes):
    out = []
    for size in reversed(sizes):
        out.append(lax.rem(index, size))
        index = lax.div(index, size)
    return out[::-1]


def one_hot_rows(targets, shape, axis):
    return (targets == lax.broadcasted_iota(jnp.int32, shape, axis)).astype(F32).astype(BF)


def frame_major_from(shape):
    row = lax.broadcasted_iota(jnp.int32, shape, 0)
    block, place, frame = digits(row, GROUP, SPAN, SPAN)
    return one_hot_rows((frame * GROUP + block) * SPAN + place, shape, 1)


def frame_major_to(shape):
    col = lax.broadcasted_iota(jnp.int32, shape, 1)
    block, place, frame = digits(col, GROUP, SPAN, SPAN)
    return one_hot_rows((frame * GROUP + block) * SPAN + place, shape, 0)


def place_major_from(shape):
    col = lax.broadcasted_iota(jnp.int32, shape, 1)
    block, place, frame = digits(col, GROUP, SPAN, SPAN)
    return one_hot_rows((place * GROUP + block) * SPAN + frame, shape, 0)


def place_major_to(shape):
    row = lax.broadcasted_iota(jnp.int32, shape, 0)
    block, place, frame = digits(row, GROUP, SPAN, SPAN)
    return one_hot_rows((place * GROUP + block) * SPAN + frame, shape, 1)


SQUARE = (GROUP * SPAN * SPAN, GROUP * SPAN * SPAN)


def split_kernel(rows_ref, out_ref):
    spread = rows_ref[0].reshape(SQUARE[0], rows_ref.shape[-1])
    moved = mm(frame_major_from(SQUARE), spread).astype(BF)
    out_ref[...] = moved.reshape(out_ref.shape)


def split_patches(rows):
    _, span, patches, width = rows.shape
    blocks = patches // span
    return pl.pallas_call(
        split_kernel,
        grid=(blocks // GROUP,),
        in_specs=[pl.BlockSpec((1, span, GROUP * span, width), lambda c: (0, 0, c, 0))],
        out_specs=pl.BlockSpec((GROUP, span * span, width), lambda c: (c, 0, 0)),
        out_shape=jax.ShapeDtypeStruct((blocks, span * span, width), BF),
        compiler_params=params(),
        cost_estimate=cost(2 * 256 * rows.size, 4 * rows.size),
        name="split_patches",
    )(rows)


def merge_kernel(rows_ref, out_ref):
    moved = mm(frame_major_to(SQUARE), rows_ref[...].reshape(SQUARE[0], rows_ref.shape[-1]))
    out_ref[0] = moved.astype(BF).reshape(out_ref.shape[1:])


def merge_patches(rows):
    blocks, rows_each, width = rows.shape
    return pl.pallas_call(
        merge_kernel,
        grid=(blocks // GROUP,),
        in_specs=[pl.BlockSpec((GROUP, rows_each, width), lambda c: (c, 0, 0))],
        out_specs=pl.BlockSpec((1, SPAN, GROUP * SPAN, width), lambda c: (0, 0, c, 0)),
        out_shape=jax.ShapeDtypeStruct((1, SPAN, blocks * SPAN, width), BF),
        compiler_params=params(),
        cost_estimate=cost(2 * 256 * rows.size, 4 * rows.size),
        name="merge_patches",
    )(rows)


def bias_kernel(bias_ref, out_ref):
    frames = out_ref.shape[-1]
    wide = jnp.broadcast_to(bias_ref[0], (frames, 2 * frames))
    rolled = pltpu.roll(wide, frames + 1, 1, stride=1, stride_axis=0)
    out_ref[0] = rolled[:, :frames]


def expand_bias(time_bias, frames):
    heads = time_bias.shape[0]
    turned = jnp.pad(time_bias[:, ::-1], ((0, 0), (0, 1))).reshape(heads, 1, 2 * frames)
    return pl.pallas_call(
        bias_kernel,
        grid=(heads,),
        in_specs=[pl.BlockSpec((1, 1, 2 * frames), lambda h: (h, 0, 0))],
        out_specs=pl.BlockSpec((1, frames, frames), lambda h: (h, 0, 0)),
        out_shape=jax.ShapeDtypeStruct((heads, frames, frames), F32),
        compiler_params=params(),
        cost_estimate=cost(heads * frames * frames * 8, 4 * heads * frames * frames),
        name="expand_bias",
    )(turned)


def gather_places(rows_ref, out_ref):
    blocks, _, width = rows_ref.shape
    order = place_major_from(SQUARE)
    run = GROUP * SPAN
    for c in range(blocks // GROUP):
        chunk = rows_ref[c * GROUP : (c + 1) * GROUP].reshape(SQUARE[0], width)
        moved = mm(order, chunk).astype(BF)
        for p in range(SPAN):
            out_ref[p, c * run : (c + 1) * run, :] = moved[p * run : (p + 1) * run, :]


def norm_parts(values):
    mean = jnp.mean(values, axis=-1, keepdims=True)
    centred = values - mean
    inv_std = lax.rsqrt(jnp.mean(centred * centred, axis=-1, keepdims=True) + 1e-05)
    return centred * inv_std, inv_std


def halves(frames):
    return lax.broadcasted_iota(jnp.int32, (frames, PAIR), 1) < PAIR // 2


def forward_kernel(
    rows_ref, gain_ref, bias_ref, w_ref, table_ref, order_ref,
    places_ref, turned_ref, proj_ref, weights_ref, att_ref, places,
):
    step = pl.program_id(0)

    @pl.when(step == 0)
    def _():
        gather_places(rows_ref, places)

    rows = places[step]
    places_ref[0] = rows
    normed, _ = norm_parts(rows.astype(F32))
    hidden = (normed * gain_ref[...] + bias_ref[...]).astype(BF)
    turned_ref[...] = mm(order_ref[...], hidden, NT).astype(BF)
    width = hidden.shape[1]
    factor = 0.125
    proj_ref[0, :, :width] = (mm(hidden, w_ref[:, :width]) * factor).astype(BF)
    proj_ref[0, :, width : 2 * width] = mm(hidden, w_ref[:, width : 2 * width]).astype(BF)
    proj_ref[0, :, 2 * width :] = mm(hidden, w_ref[:, 2 * width :]).astype(BF)
    frames = rows.shape[0]
    first = halves(frames)
    upper = lax.broadcasted_iota(jnp.int32, (PAIR, frames), 0) < PAIR // 2
    for i in range(width // PAIR):
        lanes = slice(i * PAIR, (i + 1) * PAIR)
        queries = proj_ref[0, :, lanes]
        keys = proj_ref[0, :, width + i * PAIR : width + (i + 1) * PAIR]
        vals = proj_ref[0, :, 2 * width + i * PAIR : 2 * width + (i + 1) * PAIR]
        parts = []
        for h in range(2):
            mine = jnp.where(first if h == 0 else ~first, keys, jnp.zeros_like(keys))
            scores = mm(mine, queries, NT) + table_ref[2 * i + h]
            top = jnp.max(scores, axis=0, keepdims=True)
            raised = jnp.exp(scores - top)
            total = jnp.sum(raised, axis=0, keepdims=True)
            short = (raised * (1.0 / total)).astype(BF)
            weights_ref[0, 2 * i + h] = short
            parts.append(mm(vals, short, TN))
        att_ref[0, :, lanes] = jnp.where(upper, parts[0], parts[1]).T.astype(BF)


def forward(rows, gain, bias, w_qkv, table, order):
    blocks, _, width = rows.shape
    frames = blocks * SPAN
    heads = table.shape[0]
    per = lambda *tail: pl.BlockSpec((1,) + tail, lambda p: (p,) + (0,) * len(tail))
    return pl.pallas_call(
        forward_kernel,
        grid=(SPAN,),
        in_specs=[full(rows.shape), full((1, width)), full((1, width)), full(w_qkv.shape),
                  full(table.shape), full(order.shape)],
        out_specs=[
            per(frames, width),
            pl.BlockSpec((width, frames), lambda p: (0, p)),
            per(frames, 3 * width),
            per(heads, frames, frames),
            per(frames, width),
        ],
        out_shape=[
            jax.ShapeDtypeStruct((SPAN, frames, width), BF),
            jax.ShapeDtypeStruct((width, SPAN * frames), BF),
            jax.ShapeDtypeStruct((SPAN, frames, 3 * width), BF),
            jax.ShapeDtypeStruct((SPAN, heads, frames, frames), BF),
            jax.ShapeDtypeStruct((SPAN, frames, width), BF),
        ],
        scratch_shapes=[pltpu.VMEM((SPAN, frames, width), BF)],
        compiler_params=params(),
        cost_estimate=cost(16 * 10**9, 34 * 2**20, 2**22),
        name="forward",
    )(rows, gain, bias, w_qkv, table, order)


def values_kernel(
    rows_ref, slot_ref, w_ref, weights_ref, att_ref, turned_ref, order_ref,
    grad_ref, att_grad_ref, val_grad_ref, keep_ref, send_ref, places, turned_grad, val_grads,
):
    step = pl.program_id(0)

    @pl.when(step == 0)
    def _():
        gather_places(rows_ref, places)

    frames, width = places.shape[1:]
    natural = one_hot_rows(slot_ref[...], (frames, frames), 0)
    grads = mm(natural, places[step]).astype(BF)
    grad_ref[0] = grads
    here = pl.ds(pl.multiple_of(step * frames, frames), frames)
    turned_grad[:, here] = mm(order_ref[...], grads, NT).astype(BF)
    att_grad_ref[0] = mm(grads, w_ref[...], NT).astype(BF)
    first = halves(frames)
    for i in range(width // PAIR):
        lanes = slice(i * PAIR, (i + 1) * PAIR)
        att_grad = att_grad_ref[0, :, lanes]
        parts = [mm(weights_ref[0, 2 * i + h], att_grad) for h in range(2)]
        merged = jnp.where(first, parts[0], parts[1]).astype(BF)
        val_grad_ref[0, :, lanes] = merged
        val_grads[here, lanes] = merged

    @pl.when(step == pl.num_programs(0) - 1)
    def _():
        half = width // 2
        chunk = 256
        for c in range(width // chunk):
            cols = slice(c * chunk, (c + 1) * chunk)
            after = slice(width + c * chunk, width + (c + 1) * chunk)
            term = mm(turned_ref[...], val_grads[:, cols]).astype(BF)
            keep_ref[:, cols] = term[:half]
            send_ref[:, cols] = term[half:]
            att = att_ref[:, :, cols].reshape(SPAN * frames, chunk)
            term = mm(turned_grad[...], att).astype(BF)
            keep_ref[:, after] = term[:half]
            send_ref[:, after] = term[half:]


def values_backward(rows, slot_frame, w_out, weights, att, turned, order):
    blocks, _, width = rows.shape
    frames = blocks * SPAN
    heads = weights.shape[1]
    tokens = SPAN * frames
    per = lambda *tail: pl.BlockSpec((1,) + tail, lambda p: (p,) + (0,) * len(tail))
    rows_each = jax.ShapeDtypeStruct((SPAN, frames, width), BF)
    half = jax.ShapeDtypeStruct((width // 2, 2 * width), BF)
    return pl.pallas_call(
        values_kernel,
        grid=(SPAN,),
        in_specs=[full(rows.shape), full(slot_frame.shape), full(w_out.shape), per(heads, frames, frames),
                  full(att.shape), full(turned.shape), full(order.shape)],
        out_specs=[per(frames, width), per(frames, width), per(frames, width), full(half.shape), full(half.shape)],
        out_shape=[rows_each, rows_each, rows_each, half, half],
        scratch_shapes=[
            pltpu.VMEM((SPAN, frames, width), BF),
            pltpu.VMEM((width, tokens), BF),
            pltpu.VMEM((tokens, width), BF),
        ],
        compiler_params=params(),
        cost_estimate=cost(12 * 10**9, 28 * 2**20),
        name="values_backward",
    )(rows, slot_frame, w_out, weights, att, turned, order)


def scores_kernel(
    weights_ref, proj_ref, att_grad_ref, val_grad_ref, grad_ref, places_ref, w_ref, gain_ref,
    pair_ref, out_ref, sums_ref, results,
):
    step = pl.program_id(0)
    frames, width = grad_ref.shape[1:]
    first = halves(frames)
    upper = lax.broadcasted_iota(jnp.int32, (PAIR, frames), 0) < PAIR // 2
    factor = 0.125
    for i in range(width // PAIR):
        lanes = slice(i * PAIR, (i + 1) * PAIR)
        key_lanes = slice(width + i * PAIR, width + (i + 1) * PAIR)
        queries = proj_ref[0, :, lanes]
        keys = proj_ref[0, :, key_lanes]
        vals = proj_ref[0, :, 2 * width + i * PAIR : 2 * width + (i + 1) * PAIR]
        att_grad = att_grad_ref[0, :, lanes]
        key_parts, query_parts = [], []
        for h in range(2):
            mine = jnp.where(first if h == 0 else ~first, vals, jnp.zeros_like(vals))
            weight_grad = mm(mine, att_grad, NT)
            weights = weights_ref[0, 2 * i + h].astype(F32)
            shared = jnp.sum(weight_grad * weights, axis=0, keepdims=True)
            score_grad = (weights * (weight_grad - shared)).astype(BF)
            key_parts.append(mm(score_grad, queries))
            query_parts.append(mm(keys, score_grad, TN))
        pair_ref[0, :, lanes] = (jnp.where(upper, query_parts[0], query_parts[1]) * factor).T.astype(BF)
        pair_ref[0, :, key_lanes] = jnp.where(first, key_parts[0], key_parts[1]).astype(BF)

    hidden_grad = mm(pair_ref[0], w_ref[:, : 2 * width], NT) + mm(val_grad_ref[0], w_ref[:, 2 * width :], NT)
    normed, inv_std = norm_parts(places_ref[0].astype(F32))
    scaled = hidden_grad * gain_ref[...]
    norm_grad = inv_std * (
        scaled
        - jnp.mean(scaled, axis=-1, keepdims=True)
        - normed * jnp.mean(scaled * normed, axis=-1, keepdims=True)
    )
    results[step] = (grad_ref[0].astype(F32) + norm_grad).astype(BF)
    gain_term = jnp.sum(hidden_grad * normed, axis=0, keepdims=True)
    bias_term = jnp.sum(hidden_grad, axis=0, keepdims=True)

    @pl.when(step == 0)
    def _():
        sums_ref[...] = jnp.zeros_like(sums_ref)

    sums_ref[0:1, :] += gain_term
    sums_ref[1:2, :] += bias_term

    @pl.when(step == pl.num_programs(0) - 1)
    def _():
        order = place_major_to(SQUARE)
        run = GROUP * SPAN
        for c in range(frames // run):
            chunk = results[:, c * run : (c + 1) * run, :].reshape(SQUARE[0], width)
            moved = mm(order, chunk).astype(BF)
            out_ref[c * GROUP : (c + 1) * GROUP] = moved.reshape(GROUP, SPAN * SPAN, width)


def scores_backward(weights, proj, att_grad, val_grad, grads, places, w_qkv, gain):
    _, frames, width = grads.shape
    heads = weights.shape[1]
    blocks = frames // SPAN
    per = lambda *tail: pl.BlockSpec((1,) + tail, lambda p: (p,) + (0,) * len(tail))
    return pl.pallas_call(
        scores_kernel,
        grid=(SPAN,),
        in_specs=[per(heads, frames, frames), per(frames, 3 * width), per(frames, width), per(frames, width),
                  per(frames, width), per(frames, width), full(w_qkv.shape), full((1, width))],
        out_specs=[per(frames, 2 * width), full((blocks, SPAN * SPAN, width)), full((8, width))],
        out_shape=[
            jax.ShapeDtypeStruct((SPAN, frames, 2 * width), BF),
            jax.ShapeDtypeStruct((blocks, SPAN * SPAN, width), BF),
            jax.ShapeDtypeStruct((8, width), F32),
        ],
        scratch_shapes=[pltpu.VMEM((SPAN, frames, width), BF)],
        compiler_params=params(),
        cost_estimate=cost(18 * 10**9, 34 * 2**20),
        name="scores_backward",
    )(weights, proj, att_grad, val_grad, grads, places, w_qkv, gain)


def pair_kernel(turned_ref, pair_ref, order_ref, sums_ref, keep_ref, send_ref):
    width, tokens = turned_ref.shape
    half = width // 2
    chunk = 256
    columns = pair_ref.shape[-1]
    for c in range(columns // chunk):
        cols = slice(c * chunk, (c + 1) * chunk)
        block = pair_ref[:, :, cols].reshape(tokens, chunk)
        term = mm(turned_ref[...], block).astype(BF)
        keep_ref[:, cols] = term[:half]
        send_ref[:, cols] = term[half:]
    sums = sums_ref[...]
    high = sums.astype(BF)
    low = (sums - high.astype(F32)).astype(BF)
    both = jnp.concatenate([high.astype(F32), low.astype(F32)], axis=0)
    spread = jnp.concatenate([both, jnp.zeros((PAIR - 16, width), F32)], axis=0).astype(BF)
    term = mm(order_ref[...], spread, NT).astype(BF)
    keep_ref[:, columns:] = term[:half]
    send_ref[:, columns:] = term[half:]


def pair_terms(turned, pair, order, sums):
    width, tokens = turned.shape
    columns = pair.shape[-1]
    half = jax.ShapeDtypeStruct((width // 2, columns + PAIR), BF)
    return pl.pallas_call(
        pair_kernel,
        out_shape=[half, half],
        compiler_params=params(),
        cost_estimate=cost(2 * width * tokens * columns, 14 * 2**20),
        name="pair_terms",
    )(turned, pair, order, sums)


def row_order(width):
    row = jnp.arange(width, dtype=jnp.int32)
    core, y, zh, x, zl, r = digits(row, 2, 4, 2, 4, 2, width // 128)
    core = lax.rem(core + lax.axis_index("core"), 2)
    feature = ((((y * 2 + zh) * 4 + x) * 2 + core) * 2 + zl) * (width // 128) + r
    return (feature[:, None] == jnp.arange(width, dtype=jnp.int32)[None, :]).astype(BF)


def reduce_rows(keep, send):
    got = lax.ppermute(send, "core", [(0, 1), (1, 0)])
    joined = (keep.astype(F32) + got.astype(F32)).astype(BF)
    rows, columns = joined.shape
    parts = lax.all_to_all(joined.reshape(64, rows // 64, columns), CHIPS, 0, 0, tiled=True)
    return jnp.sum(parts.astype(F32), axis=0)


def on_device(layer_input, out_grad, slot_frame, ln_gain, ln_bias, w_qkv, w_out, time_bias):
    width = layer_input.shape[-1]
    frames = slot_frame.shape[1]
    rows_in = lax.all_to_all(split_patches(layer_input), SEQ, 0, 0, tiled=True)
    rows_grad = lax.all_to_all(split_patches(out_grad), SEQ, 0, 0, tiled=True)
    table = expand_bias(time_bias, frames)
    order = row_order(width)
    gain, bias = ln_gain.reshape(1, width), ln_bias.reshape(1, width)
    places, turned, proj, weights, att = forward(rows_in, gain, bias, w_qkv, table, order)
    grads, att_grad, val_grad, keep, send = values_backward(
        rows_grad, slot_frame, w_out, weights, att, turned, order
    )
    first_sums = reduce_rows(keep, send)
    pair, out_rows, sums = scores_backward(weights, proj, att_grad, val_grad, grads, places, w_qkv, gain)
    in_grad = merge_patches(lax.all_to_all(out_rows, SEQ, 0, 0, tiled=True))
    second_sums = reduce_rows(*pair_terms(turned, pair, order, sums))
    tokens = 128 * SPAN * frames
    scale = float(tokens) ** (-0.5)
    first_sums = first_sums * scale
    second_sums = second_sums * scale
    qkv_grad = jnp.concatenate([second_sums[:, : 2 * width], first_sums[:, :width]], axis=1)
    tail = second_sums[:, 2 * width :]
    return (in_grad, qkv_grad, first_sums[:, width:], tail[:, 0] + tail[:, 8], tail[:, 1] + tail[:, 9])


def solution(mesh):
    inner = Mesh(mesh.devices.reshape(4, 2, 4, 2, 2), ("y", "zh", "x", "core", "zl"))
    every = ("y", "zh", "x", "core", "zl")
    return jax.shard_map(
        on_device,
        mesh=inner,
        in_specs=(P("zl", SEQ, None, None), P("zl", SEQ, None, None), P("zl", None), P(), P(), P(), P(), P()),
        out_specs=(P("zl", SEQ, None, None), P(every, None), P(every, None), P(every), P(every)),
        check_vma=False,
    )
```

```python
import functools

import jax
import jax.numpy as jnp
from jax import lax
from jax.experimental import pallas as pl
from jax.experimental.pallas import tpu as pltpu
from jax.sharding import Mesh, PartitionSpec as P

BF = jnp.bfloat16
F32 = jnp.float32
VMEM_BYTES = 36 * 1024 * 1024
SCORES_VMEM = 60 * 1024 * 1024
SPAN = 4
GROUP = 16
PAIR = 128
SEQ = ("y", "zh", "x", "core")
CHIPS = ("y", "zh", "x", "zl")
PLANE = ("y", "zh", "zl")

NT = (((1,), (1,)), ((), ()))
TN = (((0,), (0,)), ((), ()))


def mm(a, b, dims=(((1,), (0,)), ((), ()))):
    return lax.dot_general(a, b, dims, preferred_element_type=F32)


def params(*semantics):
    return pltpu.CompilerParams(vmem_limit_bytes=VMEM_BYTES)


def cost(flops, moved, transcendentals=0):
    return pl.CostEstimate(flops=flops, bytes_accessed=moved, transcendentals=transcendentals)


def full(shape):
    return pl.BlockSpec(shape, lambda *ids: (0,) * len(shape), pipeline_mode=pl.Buffered(1))


def digits(index, *sizes):
    out = []
    for size in reversed(sizes):
        out.append(lax.rem(index, size))
        index = lax.div(index, size)
    return out[::-1]


def one_hot_rows(targets, shape, axis):
    return (targets == lax.broadcasted_iota(jnp.int32, shape, axis)).astype(F32).astype(BF)


def frame_major_from(shape):
    row = lax.broadcasted_iota(jnp.int32, shape, 0)
    block, place, frame = digits(row, GROUP, SPAN, SPAN)
    return one_hot_rows((frame * GROUP + block) * SPAN + place, shape, 1)


def frame_major_to(shape):
    col = lax.broadcasted_iota(jnp.int32, shape, 1)
    block, place, frame = digits(col, GROUP, SPAN, SPAN)
    return one_hot_rows((frame * GROUP + block) * SPAN + place, shape, 0)


def place_major_from(shape):
    col = lax.broadcasted_iota(jnp.int32, shape, 1)
    block, place, frame = digits(col, GROUP, SPAN, SPAN)
    return one_hot_rows((place * GROUP + block) * SPAN + frame, shape, 0)


def place_major_to(shape):
    row = lax.broadcasted_iota(jnp.int32, shape, 0)
    block, place, frame = digits(row, GROUP, SPAN, SPAN)
    return one_hot_rows((place * GROUP + block) * SPAN + frame, shape, 1)


SQUARE = (GROUP * SPAN * SPAN, GROUP * SPAN * SPAN)


def split_kernel(rows_ref, out_ref):
    spread = rows_ref[0].reshape(SQUARE[0], rows_ref.shape[-1])
    moved = mm(frame_major_from(SQUARE), spread).astype(BF)
    out_ref[...] = moved.reshape(out_ref.shape)


def split_patches(rows):
    _, span, patches, width = rows.shape
    blocks = patches // span
    return pl.pallas_call(
        split_kernel,
        grid=(blocks // GROUP,),
        in_specs=[pl.BlockSpec((1, span, GROUP * span, width), lambda c: (0, 0, c, 0))],
        out_specs=pl.BlockSpec((GROUP, span * span, width), lambda c: (c, 0, 0)),
        out_shape=jax.ShapeDtypeStruct((blocks, span * span, width), BF),
        compiler_params=params(),
        cost_estimate=cost(2 * 256 * rows.size, 4 * rows.size),
        name="split_patches",
    )(rows)


def merge_kernel(rows_ref, out_ref):
    moved = mm(frame_major_to(SQUARE), rows_ref[...].reshape(SQUARE[0], rows_ref.shape[-1]))
    out_ref[0] = moved.astype(BF).reshape(out_ref.shape[1:])


def merge_patches(rows):
    blocks, rows_each, width = rows.shape
    return pl.pallas_call(
        merge_kernel,
        grid=(blocks // GROUP,),
        in_specs=[pl.BlockSpec((GROUP, rows_each, width), lambda c: (c, 0, 0))],
        out_specs=pl.BlockSpec((1, SPAN, GROUP * SPAN, width), lambda c: (0, 0, c, 0)),
        out_shape=jax.ShapeDtypeStruct((1, SPAN, blocks * SPAN, width), BF),
        compiler_params=params(),
        cost_estimate=cost(2 * 256 * rows.size, 4 * rows.size),
        name="merge_patches",
    )(rows)


def prepare_kernel(rows_ref, bias_ref, out_ref, table_ref):
    split_kernel(rows_ref, out_ref)
    heads, frames, _ = table_ref.shape
    for h in range(heads):
        wide = jnp.broadcast_to(bias_ref[h], (frames, 2 * frames))
        table_ref[h] = pltpu.roll(wide, frames + 1, 1, stride=1, stride_axis=0)[:, :frames]


def prepare(rows, time_bias, frames):
    _, span, patches, width = rows.shape
    blocks = patches // span
    steps = blocks // GROUP
    heads = time_bias.shape[0]
    turned = jnp.pad(time_bias[:, ::-1], ((0, 0), (0, 1))).reshape(heads, 1, 2 * frames)
    return pl.pallas_call(
        prepare_kernel,
        grid=(steps,),
        in_specs=[
            pl.BlockSpec((1, span, GROUP * span, width), lambda c: (0, 0, c, 0)),
            pl.BlockSpec((heads // steps, 1, 2 * frames), lambda c: (c, 0, 0)),
        ],
        out_specs=[
            pl.BlockSpec((GROUP, span * span, width), lambda c: (c, 0, 0)),
            pl.BlockSpec((heads // steps, frames, frames), lambda c: (c, 0, 0)),
        ],
        out_shape=[
            jax.ShapeDtypeStruct((blocks, span * span, width), BF),
            jax.ShapeDtypeStruct((heads, frames, frames), F32),
        ],
        compiler_params=params(),
        cost_estimate=cost(2 * 256 * rows.size, 4 * rows.size + 4 * 2**20),
        name="prepare",
    )(rows, turned)


def gather_places(rows_ref, out_ref):
    blocks, _, width = rows_ref.shape
    order = place_major_from(SQUARE)
    run = GROUP * SPAN
    for c in range(blocks // GROUP):
        chunk = rows_ref[c * GROUP : (c + 1) * GROUP].reshape(SQUARE[0], width)
        moved = mm(order, chunk).astype(BF)
        for p in range(SPAN):
            out_ref[p, c * run : (c + 1) * run, :] = moved[p * run : (p + 1) * run, :]


def norm_parts(values):
    mean = jnp.mean(values, axis=-1, keepdims=True)
    centred = values - mean
    inv_std = lax.rsqrt(jnp.mean(centred * centred, axis=-1, keepdims=True) + 1e-05)
    return centred * inv_std, inv_std


def halves(frames):
    return lax.broadcasted_iota(jnp.int32, (frames, PAIR), 1) < PAIR // 2


def forward_kernel(
    rows_ref, gain_ref, bias_ref, w_ref, table_ref,
    places_ref, turned_ref, proj_ref, weights_ref, att_ref, places,
):
    step = pl.program_id(0)

    @pl.when(step == 0)
    def _():
        gather_places(rows_ref, places)

    rows = places[step]
    places_ref[0] = rows
    normed, _ = norm_parts(rows.astype(F32))
    hidden = (normed * gain_ref[...] + bias_ref[...]).astype(BF)
    turned_ref[...] = hidden.T
    width = hidden.shape[1]
    factor = 0.125
    proj_ref[0, :, :width] = (mm(hidden, w_ref[:, :width]) * factor).astype(BF)
    proj_ref[0, :, width : 2 * width] = mm(hidden, w_ref[:, width : 2 * width]).astype(BF)
    proj_ref[0, :, 2 * width :] = mm(hidden, w_ref[:, 2 * width :]).astype(BF)
    frames = rows.shape[0]
    first = halves(frames)
    for i in range(width // PAIR):
        lanes = slice(i * PAIR, (i + 1) * PAIR)
        queries = proj_ref[0, :, lanes]
        keys = proj_ref[0, :, width + i * PAIR : width + (i + 1) * PAIR]
        vals = proj_ref[0, :, 2 * width + i * PAIR : 2 * width + (i + 1) * PAIR]
        parts = []
        for h in range(2):
            mine = jnp.where(first if h == 0 else ~first, keys, jnp.zeros_like(keys))
            scores = mm(mine, queries, NT) + table_ref[2 * i + h]
            top = jnp.max(scores, axis=0, keepdims=True)
            raised = jnp.exp(scores - top)
            total = jnp.sum(raised, axis=0, keepdims=True)
            short = (raised * (1.0 / total)).astype(BF)
            weights_ref[0, 2 * i + h] = short
            parts.append(mm(short, vals, TN))
        att_ref[0, :, lanes] = jnp.where(first, parts[0], parts[1]).astype(BF)


def forward(rows, gain, bias, w_qkv, table):
    blocks, _, width = rows.shape
    frames = blocks * SPAN
    heads = table.shape[0]
    per = lambda *tail: pl.BlockSpec((1,) + tail, lambda p: (p,) + (0,) * len(tail))
    return pl.pallas_call(
        forward_kernel,
        grid=(SPAN,),
        in_specs=[full(rows.shape), full((1, width)), full((1, width)), full(w_qkv.shape),
                  full(table.shape)],
        out_specs=[
            per(frames, width),
            pl.BlockSpec((width, frames), lambda p: (0, p)),
            per(frames, 3 * width),
            per(heads, frames, frames),
            per(frames, width),
        ],
        out_shape=[
            jax.ShapeDtypeStruct((SPAN, frames, width), BF),
            jax.ShapeDtypeStruct((width, SPAN * frames), BF),
            jax.ShapeDtypeStruct((SPAN, frames, 3 * width), BF),
            jax.ShapeDtypeStruct((SPAN, heads, frames, frames), BF),
            jax.ShapeDtypeStruct((SPAN, frames, width), BF),
        ],
        scratch_shapes=[pltpu.VMEM((SPAN, frames, width), BF)],
        compiler_params=params(),
        cost_estimate=cost(16 * 10**9, 34 * 2**20, 2**22),
        name="forward",
    )(rows, gain, bias, w_qkv, table)


def place_rows(terms, order_ref, line, keep_ref, send_ref, cols):
    count = order_ref.shape[1]
    half = count // 2
    for i in range(0, count, 2):
        pair = []
        for j in (i, i + 1):
            start = pl.multiple_of(order_ref[line, j] * 8, 8)
            pair.append(terms[pl.ds(start, 8), :])
        rows = jnp.concatenate(pair, axis=0).astype(BF)
        target, at = (keep_ref, i) if i < half else (send_ref, i - half)
        target[at * 8 : at * 8 + 16, cols] = rows


def values_kernel(
    order_ref, rows_ref, slot_ref, w_ref, weights_ref, att_ref, turned_ref,
    grad_ref, att_grad_ref, val_grad_ref, keep_ref, send_ref, places, turned_grad, val_grads, terms,
):
    step = pl.program_id(0)

    @pl.when(step == 0)
    def _():
        gather_places(rows_ref, places)

    frames, width = places.shape[1:]
    natural = one_hot_rows(slot_ref[...], (frames, frames), 0)
    grads = mm(natural, places[step]).astype(BF)
    grad_ref[0] = grads
    here = pl.ds(pl.multiple_of(step * frames, frames), frames)
    turned_grad[:, here] = grads.T
    att_grad_ref[0] = mm(grads, w_ref[...], NT).astype(BF)
    first = halves(frames)
    for i in range(width // PAIR):
        lanes = slice(i * PAIR, (i + 1) * PAIR)
        att_grad = att_grad_ref[0, :, lanes]
        parts = [mm(weights_ref[0, 2 * i + h], att_grad) for h in range(2)]
        merged = jnp.where(first, parts[0], parts[1]).astype(BF)
        val_grad_ref[0, :, lanes] = merged
        val_grads[here, lanes] = merged

    @pl.when(step == pl.num_programs(0) - 1)
    def _():
        chunk = terms.shape[1]
        for c in range(width // chunk):
            cols = slice(c * chunk, (c + 1) * chunk)
            after = slice(width + c * chunk, width + (c + 1) * chunk)
            terms[...] = mm(turned_ref[...], val_grads[:, cols])
            place_rows(terms, order_ref, 0, keep_ref, send_ref, cols)
            terms[...] = mm(turned_grad[...], att_ref[:, :, cols].reshape(SPAN * frames, chunk))
            place_rows(terms, order_ref, 0, keep_ref, send_ref, after)


def values_backward(order, rows, slot_frame, w_out, weights, att, turned):
    blocks, _, width = rows.shape
    frames = blocks * SPAN
    heads = weights.shape[1]
    tokens = SPAN * frames
    per = lambda *tail: pl.BlockSpec((1,) + tail, lambda p, _: (p,) + (0,) * len(tail))
    rows_each = jax.ShapeDtypeStruct((SPAN, frames, width), BF)
    half = jax.ShapeDtypeStruct((width // 2, 2 * width), BF)
    return pl.pallas_call(
        values_kernel,
        grid_spec=pltpu.PrefetchScalarGridSpec(
            num_scalar_prefetch=1,
            grid=(SPAN,),
            in_specs=[full(rows.shape), full(slot_frame.shape), full(w_out.shape), per(heads, frames, frames),
                      full(att.shape), full(turned.shape)],
            out_specs=[per(frames, width), per(frames, width), per(frames, width), full(half.shape), full(half.shape)],
            scratch_shapes=[
                pltpu.VMEM((SPAN, frames, width), BF),
                pltpu.VMEM((width, tokens), BF),
                pltpu.VMEM((tokens, width), BF),
                pltpu.VMEM((width, 256), F32),
            ],
        ),
        out_shape=[rows_each, rows_each, rows_each, half, half],
        compiler_params=params(),
        cost_estimate=cost(12 * 10**9, 28 * 2**20),
        name="values_backward",
    )(order, rows, slot_frame, w_out, weights, att, turned)


def scores_kernel(
    order_ref, joined_ref, weights_ref, proj_ref, att_grad_ref, val_grad_ref, grad_ref, places_ref, w_ref, gain_ref,
    turned_ref, out_ref, keep_ref, send_ref, results, pairs, sums, terms,
):
    step = pl.program_id(0)
    frames, width = grad_ref.shape[1:]
    first = halves(frames)
    factor = 0.125
    here = pl.ds(pl.multiple_of(step * frames, frames), frames)
    for i in range(width // PAIR):
        lanes = slice(i * PAIR, (i + 1) * PAIR)
        key_lanes = slice(width + i * PAIR, width + (i + 1) * PAIR)
        queries = proj_ref[0, :, lanes]
        keys = proj_ref[0, :, key_lanes]
        vals = proj_ref[0, :, 2 * width + i * PAIR : 2 * width + (i + 1) * PAIR]
        att_grad = att_grad_ref[0, :, lanes]
        key_parts, query_parts = [], []
        for h in range(2):
            mine = jnp.where(first if h == 0 else ~first, vals, jnp.zeros_like(vals))
            weight_grad = mm(mine, att_grad, NT)
            weights = weights_ref[0, 2 * i + h].astype(F32)
            shared = jnp.sum(weight_grad * weights, axis=0, keepdims=True)
            score_grad = (weights * (weight_grad - shared)).astype(BF)
            key_parts.append(mm(score_grad, queries))
            query_parts.append(mm(score_grad, keys, TN))
        pairs[here, lanes] = (jnp.where(first, query_parts[0], query_parts[1]) * factor).astype(BF)
        pairs[here, key_lanes] = jnp.where(first, key_parts[0], key_parts[1]).astype(BF)

    hidden_grad = mm(pairs[here, :], w_ref[:, : 2 * width], NT) + mm(val_grad_ref[0], w_ref[:, 2 * width :], NT)
    normed, inv_std = norm_parts(places_ref[0].astype(F32))
    scaled = hidden_grad * gain_ref[...]
    norm_grad = inv_std * (
        scaled
        - jnp.mean(scaled, axis=-1, keepdims=True)
        - normed * jnp.mean(scaled * normed, axis=-1, keepdims=True)
    )
    results[step] = (grad_ref[0].astype(F32) + norm_grad).astype(BF)
    gain_term = jnp.sum(hidden_grad * normed, axis=0, keepdims=True)
    bias_term = jnp.sum(hidden_grad, axis=0, keepdims=True)

    @pl.when(step == 0)
    def _():
        sums[...] = jnp.zeros_like(sums)

    sums[0:1, :] += gain_term
    sums[1:2, :] += bias_term

    @pl.when(step == pl.num_programs(0) - 1)
    def _():
        order = place_major_to(SQUARE)
        run = GROUP * SPAN
        for c in range(frames // run):
            chunk = results[:, c * run : (c + 1) * run, :].reshape(SQUARE[0], width)
            moved = mm(order, chunk).astype(BF)
            out_ref[c * GROUP : (c + 1) * GROUP] = moved.reshape(GROUP, SPAN * SPAN, width)
        chunk = terms.shape[1]
        for at in range(0, 2 * width, chunk):
            terms[...] = mm(turned_ref[...], pairs[:, at : at + chunk])
            place_rows(terms, order_ref, 1, keep_ref, send_ref, slice(at, at + chunk))
        terms[:, :PAIR] = jnp.concatenate([sums[...]] * (PAIR // sums.shape[0]), axis=0).T
        place_rows(terms.at[:, :PAIR], order_ref, 1, keep_ref, send_ref, slice(2 * width, 2 * width + PAIR))


def scores_backward(order, joined, weights, proj, att_grad, val_grad, grads, places, w_qkv, gain, turned):
    _, frames, width = grads.shape
    heads = weights.shape[1]
    blocks = frames // SPAN
    tokens = SPAN * frames
    per = lambda *tail: pl.BlockSpec((1,) + tail, lambda p, _: (p,) + (0,) * len(tail))
    half = jax.ShapeDtypeStruct((width // 2, 2 * width + PAIR), BF)
    outs = [jax.ShapeDtypeStruct((blocks, SPAN * SPAN, width), BF), half, half]
    return pl.pallas_call(
        scores_kernel,
        grid_spec=pltpu.PrefetchScalarGridSpec(
            num_scalar_prefetch=1,
            grid=(SPAN,),
            in_specs=[pl.BlockSpec(memory_space=pl.ANY), per(heads, frames, frames), per(frames, 3 * width),
                      per(frames, width), per(frames, width), per(frames, width), per(frames, width),
                      full(w_qkv.shape), full((1, width)), full(turned.shape)],
            out_specs=[full(o.shape) for o in outs],
            scratch_shapes=[
                pltpu.VMEM((SPAN, frames, width), BF),
                pltpu.VMEM((tokens, 2 * width), BF),
                pltpu.VMEM((8, width), F32),
                pltpu.VMEM((width, 256), F32),
            ],
        ),
        out_shape=outs,
        compiler_params=pltpu.CompilerParams(vmem_limit_bytes=SCORES_VMEM),
        cost_estimate=cost(24 * 10**9, 34 * 2**20),
        name="scores_backward",
    )(order, joined, weights, proj, att_grad, val_grad, grads, places, w_qkv, gain, turned)


def total_kernel(parts_ref, *refs):
    total_ref = refs[len(refs) // 2]
    total_ref[...] = jnp.sum(parts_ref[...].astype(F32), axis=0)


def sum_parts(parts, *passed):
    anywhere = [pl.BlockSpec(memory_space=pltpu.HBM)] * len(passed)
    here = pl.BlockSpec(memory_space=pltpu.VMEM)
    return pl.pallas_call(
        total_kernel,
        in_specs=[here] + anywhere,
        out_specs=[here] + anywhere,
        out_shape=[jax.ShapeDtypeStruct(parts.shape[1:], F32)]
        + [jax.ShapeDtypeStruct(p.shape, p.dtype) for p in passed],
        input_output_aliases={i + 1: i + 1 for i in range(len(passed))},
        compiler_params=params(),
        cost_estimate=cost(parts.size, 2 * parts.size),
        name="sum_parts",
    )(parts, *passed)


def gray(place):
    return place ^ (place >> 1)


def row_orders():
    place = jnp.arange(128, dtype=jnp.int32)
    core = lax.axis_index("core") ^ (place >> 6)

    def block(y, zh, x, zl):
        return (((y * 2 + zh) * 4 + x) * 2 + core) * 2 + zl

    direct = block(*digits(place & 63, 4, 2, 4, 2))
    one, two, y, zh, zl = digits(place & 63, 2, 2, 4, 2, 2)
    mask = jnp.where(core == 0, one + 2 * two, 2 * one + two)
    x = gray(gray(lax.axis_index("x")) ^ mask)
    return jnp.stack([direct, block(y, zh, x, zl)]).astype(jnp.int32)


def neighbours(step):
    pairs = []
    for place in range(4):
        for core in range(2):
            mask = 1 if step == core else 2
            pairs.append((place * 2 + core, gray(gray(place) ^ mask) * 2 + core))
    return pairs


def after_kernel(held_ref, other_ref, out_ref):
    del held_ref, other_ref, out_ref


def after(held, other):
    anywhere = pl.BlockSpec(memory_space=pltpu.HBM)
    return pl.pallas_call(
        after_kernel,
        in_specs=[anywhere, anywhere],
        out_specs=anywhere,
        out_shape=jax.ShapeDtypeStruct(held.shape, held.dtype),
        input_output_aliases={0: 0},
        name="after",
    )(held, other)


def add(a, b):
    return (a.astype(F32) + b.astype(F32)).astype(BF)


def halve(held, step):
    half = held.shape[0] // 2
    return add(held[:half], lax.ppermute(held[half:], ("x", "core"), neighbours(step)))


def join_cores(keep, send):
    return add(keep, lax.ppermute(send, "core", [(0, 1), (1, 0)]))


def to_owners(joined, axes, count):
    rows, columns = joined.shape
    return lax.all_to_all(joined.reshape(count, rows // count, columns), axes, 0, 0, tiled=True)


def on_device(layer_input, out_grad, slot_frame, ln_gain, ln_bias, w_qkv, w_out, time_bias):
    width = layer_input.shape[-1]
    frames = slot_frame.shape[1]
    rows_in = lax.all_to_all(split_patches(layer_input), SEQ, 0, 0, tiled=True)
    split_grad, table = prepare(out_grad, time_bias, frames)
    rows_grad = lax.all_to_all(split_grad, SEQ, 0, 0, tiled=True)
    orders = row_orders()
    gain, bias = ln_gain.reshape(1, width), ln_bias.reshape(1, width)
    places, turned, proj, weights, att = forward(rows_in, gain, bias, w_qkv, table)
    grads, att_grad, val_grad, keep, send = values_backward(
        orders, rows_grad, slot_frame, w_out, weights, att, turned
    )
    joined = join_cores(keep, send)
    parts = to_owners(joined, CHIPS, 64)
    out_rows, keep, send = scores_backward(
        orders, joined, weights, proj, att_grad, val_grad, grads, places, w_qkv, gain, turned
    )
    first_sums, out_rows, keep, send = sum_parts(parts, out_rows, keep, send)
    out_parts = lax.all_to_all(out_rows, SEQ, 0, 0, tiled=True)
    held = halve(halve(join_cores(keep, send), 0), 1)
    in_grad = merge_patches(out_parts)
    held = after(held, out_parts)
    second_sums = jnp.sum(to_owners(held, PLANE, 16).astype(F32), axis=0)
    tokens = 128 * SPAN * frames
    scale = float(tokens) ** (-0.5)
    first_sums = first_sums * scale
    second_sums = second_sums * scale
    qkv_grad = jnp.concatenate([second_sums[:, : 2 * width], first_sums[:, :width]], axis=1)
    tail = second_sums[:, 2 * width :]
    return (in_grad, qkv_grad, first_sums[:, width:], tail[:, 0], tail[:, 1])


def solution(mesh):
    inner = Mesh(mesh.devices.reshape(4, 2, 4, 2, 2), ("y", "zh", "x", "core", "zl"))
    every = ("y", "zh", "x", "core", "zl")
    return jax.shard_map(
        on_device,
        mesh=inner,
        in_specs=(P("zl", SEQ, None, None), P("zl", SEQ, None, None), P("zl", None), P(), P(), P(), P(), P()),
        out_specs=(P("zl", SEQ, None, None), P(every, None), P(every, None), P(every), P(every)),
        check_vma=False,
    )
```

```python
import functools

import jax
import jax.numpy as jnp
from jax import lax
from jax.experimental import pallas as pl
from jax.experimental.pallas import tpu as pltpu
from jax.sharding import Mesh, PartitionSpec as P

BF = jnp.bfloat16
F32 = jnp.float32
VMEM_BYTES = 36 * 1024 * 1024
SCORES_VMEM = 60 * 1024 * 1024
SPAN = 4
GROUP = 16
PAIR = 128
SEQ = ("y", "zh", "x", "core")
CHIPS = ("y", "zh", "x", "zl")
PLANE = ("y", "zh", "zl")

NT = (((1,), (1,)), ((), ()))
TN = (((0,), (0,)), ((), ()))


def mm(a, b, dims=(((1,), (0,)), ((), ()))):
    return lax.dot_general(a, b, dims, preferred_element_type=F32)


def params(*semantics):
    return pltpu.CompilerParams(vmem_limit_bytes=VMEM_BYTES)


def cost(flops, moved, transcendentals=0):
    return pl.CostEstimate(flops=flops, bytes_accessed=moved, transcendentals=transcendentals)


def full(shape):
    return pl.BlockSpec(shape, lambda *ids: (0,) * len(shape), pipeline_mode=pl.Buffered(1))


def digits(index, *sizes):
    out = []
    for size in reversed(sizes):
        out.append(lax.rem(index, size))
        index = lax.div(index, size)
    return out[::-1]


def one_hot_rows(targets, shape, axis):
    return (targets == lax.broadcasted_iota(jnp.int32, shape, axis)).astype(F32).astype(BF)


def frame_major_from(shape):
    row = lax.broadcasted_iota(jnp.int32, shape, 0)
    block, place, frame = digits(row, GROUP, SPAN, SPAN)
    return one_hot_rows((frame * GROUP + block) * SPAN + place, shape, 1)


def frame_major_to(shape):
    col = lax.broadcasted_iota(jnp.int32, shape, 1)
    block, place, frame = digits(col, GROUP, SPAN, SPAN)
    return one_hot_rows((frame * GROUP + block) * SPAN + place, shape, 0)


def place_major_from(shape):
    col = lax.broadcasted_iota(jnp.int32, shape, 1)
    block, place, frame = digits(col, GROUP, SPAN, SPAN)
    return one_hot_rows((place * GROUP + block) * SPAN + frame, shape, 0)


def place_major_to(shape):
    row = lax.broadcasted_iota(jnp.int32, shape, 0)
    block, place, frame = digits(row, GROUP, SPAN, SPAN)
    return one_hot_rows((place * GROUP + block) * SPAN + frame, shape, 1)


SQUARE = (GROUP * SPAN * SPAN, GROUP * SPAN * SPAN)


def split_kernel(rows_ref, out_ref):
    spread = rows_ref[0].reshape(SQUARE[0], rows_ref.shape[-1])
    moved = mm(frame_major_from(SQUARE), spread).astype(BF)
    out_ref[...] = moved.reshape(out_ref.shape)


def split_patches(rows):
    _, span, patches, width = rows.shape
    blocks = patches // span
    return pl.pallas_call(
        split_kernel,
        grid=(blocks // GROUP,),
        in_specs=[pl.BlockSpec((1, span, GROUP * span, width), lambda c: (0, 0, c, 0))],
        out_specs=pl.BlockSpec((GROUP, span * span, width), lambda c: (c, 0, 0)),
        out_shape=jax.ShapeDtypeStruct((blocks, span * span, width), BF),
        compiler_params=params(),
        cost_estimate=cost(2 * 256 * rows.size, 4 * rows.size),
        name="split_patches",
    )(rows)


def merge_kernel(rows_ref, out_ref):
    moved = mm(frame_major_to(SQUARE), rows_ref[...].reshape(SQUARE[0], rows_ref.shape[-1]))
    out_ref[0] = moved.astype(BF).reshape(out_ref.shape[1:])


def merge_patches(rows):
    blocks, rows_each, width = rows.shape
    return pl.pallas_call(
        merge_kernel,
        grid=(blocks // GROUP,),
        in_specs=[pl.BlockSpec((GROUP, rows_each, width), lambda c: (c, 0, 0))],
        out_specs=pl.BlockSpec((1, SPAN, GROUP * SPAN, width), lambda c: (0, 0, c, 0)),
        out_shape=jax.ShapeDtypeStruct((1, SPAN, blocks * SPAN, width), BF),
        compiler_params=params(),
        cost_estimate=cost(2 * 256 * rows.size, 4 * rows.size),
        name="merge_patches",
    )(rows)


def prepare_kernel(rows_ref, bias_ref, out_ref, table_ref):
    split_kernel(rows_ref, out_ref)
    heads, frames, _ = table_ref.shape
    for h in range(heads):
        wide = jnp.broadcast_to(bias_ref[h], (frames, 2 * frames))
        table_ref[h] = pltpu.roll(wide, frames + 1, 1, stride=1, stride_axis=0)[:, :frames]


def prepare(rows, time_bias, frames):
    _, span, patches, width = rows.shape
    blocks = patches // span
    steps = blocks // GROUP
    heads = time_bias.shape[0]
    turned = jnp.pad(time_bias[:, ::-1], ((0, 0), (0, 1))).reshape(heads, 1, 2 * frames)
    return pl.pallas_call(
        prepare_kernel,
        grid=(steps,),
        in_specs=[
            pl.BlockSpec((1, span, GROUP * span, width), lambda c: (0, 0, c, 0)),
            pl.BlockSpec((heads // steps, 1, 2 * frames), lambda c: (c, 0, 0)),
        ],
        out_specs=[
            pl.BlockSpec((GROUP, span * span, width), lambda c: (c, 0, 0)),
            pl.BlockSpec((heads // steps, frames, frames), lambda c: (c, 0, 0)),
        ],
        out_shape=[
            jax.ShapeDtypeStruct((blocks, span * span, width), BF),
            jax.ShapeDtypeStruct((heads, frames, frames), F32),
        ],
        compiler_params=params(),
        cost_estimate=cost(2 * 256 * rows.size, 4 * rows.size + 4 * 2**20),
        name="prepare",
    )(rows, turned)


def gather_places(rows_ref, out_ref):
    blocks, _, width = rows_ref.shape
    order = place_major_from(SQUARE)
    run = GROUP * SPAN
    for c in range(blocks // GROUP):
        chunk = rows_ref[c * GROUP : (c + 1) * GROUP].reshape(SQUARE[0], width)
        moved = mm(order, chunk).astype(BF)
        for p in range(SPAN):
            out_ref[p, c * run : (c + 1) * run, :] = moved[p * run : (p + 1) * run, :]


def norm_parts(values):
    mean = jnp.mean(values, axis=-1, keepdims=True)
    centred = values - mean
    inv_std = lax.rsqrt(jnp.mean(centred * centred, axis=-1, keepdims=True) + 1e-05)
    return centred * inv_std, inv_std


def halves(frames):
    return lax.broadcasted_iota(jnp.int32, (frames, PAIR), 1) < PAIR // 2


def forward_kernel(
    rows_ref, gain_ref, bias_ref, w_ref, table_ref,
    places_ref, turned_ref, proj_ref, weights_ref, natural_ref, att_ref, places,
):
    step = pl.program_id(0)

    @pl.when(step == 0)
    def _():
        gather_places(rows_ref, places)

    rows = places[step]
    places_ref[0] = rows
    normed, _ = norm_parts(rows.astype(F32))
    hidden = (normed * gain_ref[...] + bias_ref[...]).astype(BF)
    turned_ref[...] = hidden.T
    width = hidden.shape[1]
    factor = 0.125
    proj_ref[0, :, :width] = (mm(hidden, w_ref[:, :width]) * factor).astype(BF)
    proj_ref[0, :, width : 2 * width] = mm(hidden, w_ref[:, width : 2 * width]).astype(BF)
    proj_ref[0, :, 2 * width :] = mm(hidden, w_ref[:, 2 * width :]).astype(BF)
    frames = rows.shape[0]
    first = halves(frames)
    for i in range(width // PAIR):
        lanes = slice(i * PAIR, (i + 1) * PAIR)
        queries = proj_ref[0, :, lanes]
        keys = proj_ref[0, :, width + i * PAIR : width + (i + 1) * PAIR]
        vals = proj_ref[0, :, 2 * width + i * PAIR : 2 * width + (i + 1) * PAIR]
        parts = []
        for h in range(2):
            mine = jnp.where(first if h == 0 else ~first, keys, jnp.zeros_like(keys))
            scores = mm(mine, queries, NT) + table_ref[2 * i + h]
            top = jnp.max(scores, axis=0, keepdims=True)
            raised = jnp.exp(scores - top)
            total = jnp.sum(raised, axis=0, keepdims=True)
            short = (raised * (1.0 / total)).astype(BF)
            weights_ref[0, 2 * i + h] = short
            natural = short.T
            natural_ref[0, 2 * i + h] = natural
            parts.append(mm(natural, vals))
        att_ref[0, :, lanes] = jnp.where(first, parts[0], parts[1]).astype(BF)


def forward(rows, gain, bias, w_qkv, table):
    blocks, _, width = rows.shape
    frames = blocks * SPAN
    heads = table.shape[0]
    per = lambda *tail: pl.BlockSpec((1,) + tail, lambda p: (p,) + (0,) * len(tail))
    return pl.pallas_call(
        forward_kernel,
        grid=(SPAN,),
        in_specs=[full(rows.shape), full((1, width)), full((1, width)), full(w_qkv.shape),
                  full(table.shape)],
        out_specs=[
            per(frames, width),
            pl.BlockSpec((width, frames), lambda p: (0, p)),
            per(frames, 3 * width),
            per(heads, frames, frames),
            per(heads, frames, frames),
            per(frames, width),
        ],
        out_shape=[
            jax.ShapeDtypeStruct((SPAN, frames, width), BF),
            jax.ShapeDtypeStruct((width, SPAN * frames), BF),
            jax.ShapeDtypeStruct((SPAN, frames, 3 * width), BF),
            jax.ShapeDtypeStruct((SPAN, heads, frames, frames), BF),
            jax.ShapeDtypeStruct((SPAN, heads, frames, frames), BF),
            jax.ShapeDtypeStruct((SPAN, frames, width), BF),
        ],
        scratch_shapes=[pltpu.VMEM((SPAN, frames, width), BF)],
        compiler_params=params(),
        cost_estimate=cost(16 * 10**9, 34 * 2**20, 2**22),
        name="forward",
    )(rows, gain, bias, w_qkv, table)


def place_rows(terms, order_ref, line, keep_ref, send_ref, cols):
    count = order_ref.shape[1]
    half = count // 2
    for i in range(0, count, 2):
        pair = []
        for j in (i, i + 1):
            start = pl.multiple_of(order_ref[line, j] * 8, 8)
            pair.append(terms[pl.ds(start, 8), :])
        rows = jnp.concatenate(pair, axis=0).astype(BF)
        target, at = (keep_ref, i) if i < half else (send_ref, i - half)
        target[at * 8 : at * 8 + 16, cols] = rows


def values_kernel(
    order_ref, rows_ref, slot_ref, w_ref, weights_ref, att_ref, turned_ref,
    grad_ref, att_grad_ref, val_grad_ref, keep_ref, send_ref, places, turned_grad, val_grads, terms,
):
    step = pl.program_id(0)

    @pl.when(step == 0)
    def _():
        gather_places(rows_ref, places)

    frames, width = places.shape[1:]
    natural = one_hot_rows(slot_ref[...], (frames, frames), 0)
    grads = mm(natural, places[step]).astype(BF)
    grad_ref[0] = grads
    here = pl.ds(pl.multiple_of(step * frames, frames), frames)
    turned_grad[:, here] = grads.T
    att_grad_ref[0] = mm(grads, w_ref[...], NT).astype(BF)
    first = halves(frames)
    for i in range(width // PAIR):
        lanes = slice(i * PAIR, (i + 1) * PAIR)
        att_grad = att_grad_ref[0, :, lanes]
        parts = [mm(weights_ref[0, 2 * i + h], att_grad) for h in range(2)]
        merged = jnp.where(first, parts[0], parts[1]).astype(BF)
        val_grad_ref[0, :, lanes] = merged
        val_grads[here, lanes] = merged

    @pl.when(step == pl.num_programs(0) - 1)
    def _():
        chunk = terms.shape[1]
        for c in range(width // chunk):
            cols = slice(c * chunk, (c + 1) * chunk)
            after = slice(width + c * chunk, width + (c + 1) * chunk)
            terms[...] = mm(turned_ref[...], val_grads[:, cols])
            place_rows(terms, order_ref, 0, keep_ref, send_ref, cols)
            terms[...] = mm(turned_grad[...], att_ref[:, :, cols].reshape(SPAN * frames, chunk))
            place_rows(terms, order_ref, 0, keep_ref, send_ref, after)


def values_backward(order, rows, slot_frame, w_out, weights, att, turned):
    blocks, _, width = rows.shape
    frames = blocks * SPAN
    heads = weights.shape[1]
    tokens = SPAN * frames
    per = lambda *tail: pl.BlockSpec((1,) + tail, lambda p, _: (p,) + (0,) * len(tail))
    rows_each = jax.ShapeDtypeStruct((SPAN, frames, width), BF)
    half = jax.ShapeDtypeStruct((width // 2, 2 * width), BF)
    return pl.pallas_call(
        values_kernel,
        grid_spec=pltpu.PrefetchScalarGridSpec(
            num_scalar_prefetch=1,
            grid=(SPAN,),
            in_specs=[full(rows.shape), full(slot_frame.shape), full(w_out.shape), per(heads, frames, frames),
                      full(att.shape), full(turned.shape)],
            out_specs=[per(frames, width), per(frames, width), per(frames, width), full(half.shape), full(half.shape)],
            scratch_shapes=[
                pltpu.VMEM((SPAN, frames, width), BF),
                pltpu.VMEM((width, tokens), BF),
                pltpu.VMEM((tokens, width), BF),
                pltpu.VMEM((width, 256), F32),
            ],
        ),
        out_shape=[rows_each, rows_each, rows_each, half, half],
        compiler_params=params(),
        cost_estimate=cost(12 * 10**9, 28 * 2**20),
        name="values_backward",
    )(order, rows, slot_frame, w_out, weights, att, turned)


def scores_kernel(
    order_ref, joined_ref, weights_ref, natural_ref, proj_ref, att_grad_ref, val_grad_ref, grad_ref, places_ref, w_far, gain_ref,
    turned_far, out_ref, keep_ref, send_ref, results, pairs, sums, terms, w_ref, turned_ref, arrived,
):
    step = pl.program_id(0)
    copies = [
        pltpu.make_async_copy(w_far, w_ref, arrived.at[0]),
        pltpu.make_async_copy(turned_far, turned_ref, arrived.at[1]),
    ]

    @pl.when(step == 0)
    def _():
        for copy in copies:
            copy.start()

    frames, width = grad_ref.shape[1:]
    first = halves(frames)
    factor = 0.125
    here = pl.ds(pl.multiple_of(step * frames, frames), frames)
    for i in range(width // PAIR):
        lanes = slice(i * PAIR, (i + 1) * PAIR)
        key_lanes = slice(width + i * PAIR, width + (i + 1) * PAIR)
        queries = proj_ref[0, :, lanes]
        keys = proj_ref[0, :, key_lanes]
        vals = proj_ref[0, :, 2 * width + i * PAIR : 2 * width + (i + 1) * PAIR]
        att_grad = att_grad_ref[0, :, lanes]
        key_parts, query_parts = [], []
        for h in range(2):
            mine = jnp.where(first if h == 0 else ~first, vals, jnp.zeros_like(vals))
            weight_grad = mm(mine, att_grad, NT)
            weights = weights_ref[0, 2 * i + h].astype(F32)
            shared = jnp.sum(weight_grad * weights, axis=0, keepdims=True)
            score_grad = (weights * (weight_grad - shared)).astype(BF)
            key_parts.append(mm(score_grad, queries))
            weight_grad = mm(jnp.where(first if h == 0 else ~first, att_grad, jnp.zeros_like(att_grad)), vals, NT)
            weights = natural_ref[0, 2 * i + h].astype(F32)
            shared = jnp.sum(weight_grad * weights, axis=1, keepdims=True)
            query_parts.append(mm((weights * (weight_grad - shared)).astype(BF), keys))
        pairs[here, lanes] = (jnp.where(first, query_parts[0], query_parts[1]) * factor).astype(BF)
        pairs[here, key_lanes] = jnp.where(first, key_parts[0], key_parts[1]).astype(BF)

    @pl.when(step == 0)
    def _():
        for copy in copies:
            copy.wait()

    hidden_grad = mm(pairs[here, :], w_ref[:, : 2 * width], NT) + mm(val_grad_ref[0], w_ref[:, 2 * width :], NT)
    normed, inv_std = norm_parts(places_ref[0].astype(F32))
    scaled = hidden_grad * gain_ref[...]
    norm_grad = inv_std * (
        scaled
        - jnp.mean(scaled, axis=-1, keepdims=True)
        - normed * jnp.mean(scaled * normed, axis=-1, keepdims=True)
    )
    results[step] = (grad_ref[0].astype(F32) + norm_grad).astype(BF)
    gain_term = jnp.sum(hidden_grad * normed, axis=0, keepdims=True)
    bias_term = jnp.sum(hidden_grad, axis=0, keepdims=True)

    @pl.when(step == 0)
    def _():
        sums[...] = jnp.zeros_like(sums)

    sums[0:1, :] += gain_term
    sums[1:2, :] += bias_term

    @pl.when(step == pl.num_programs(0) - 1)
    def _():
        order = place_major_to(SQUARE)
        run = GROUP * SPAN
        for c in range(frames // run):
            chunk = results[:, c * run : (c + 1) * run, :].reshape(SQUARE[0], width)
            moved = mm(order, chunk).astype(BF)
            out_ref[c * GROUP : (c + 1) * GROUP] = moved.reshape(GROUP, SPAN * SPAN, width)
        chunk = terms.shape[1]
        for at in range(0, 2 * width, chunk):
            terms[...] = mm(turned_ref[...], pairs[:, at : at + chunk])
            place_rows(terms, order_ref, 1, keep_ref, send_ref, slice(at, at + chunk))
        terms[:, :PAIR] = jnp.concatenate([sums[...]] * (PAIR // sums.shape[0]), axis=0).T
        place_rows(terms.at[:, :PAIR], order_ref, 1, keep_ref, send_ref, slice(2 * width, 2 * width + PAIR))


def scores_backward(order, joined, weights, natural, proj, att_grad, val_grad, grads, places, w_qkv, gain, turned):
    _, frames, width = grads.shape
    heads = weights.shape[1]
    blocks = frames // SPAN
    tokens = SPAN * frames
    per = lambda *tail: pl.BlockSpec((1,) + tail, lambda p, _: (p,) + (0,) * len(tail))
    half = jax.ShapeDtypeStruct((width // 2, 2 * width + PAIR), BF)
    outs = [jax.ShapeDtypeStruct((blocks, SPAN * SPAN, width), BF), half, half]
    return pl.pallas_call(
        scores_kernel,
        grid_spec=pltpu.PrefetchScalarGridSpec(
            num_scalar_prefetch=1,
            grid=(SPAN,),
            in_specs=[pl.BlockSpec(memory_space=pl.ANY), per(heads, frames, frames), per(heads, frames, frames),
                      per(frames, 3 * width),
                      per(frames, width), per(frames, width), per(frames, width), per(frames, width),
                      pl.BlockSpec(memory_space=pl.ANY), full((1, width)), pl.BlockSpec(memory_space=pl.ANY)],
            out_specs=[full(o.shape) for o in outs],
            scratch_shapes=[
                pltpu.VMEM((SPAN, frames, width), BF),
                pltpu.VMEM((tokens, 2 * width), BF),
                pltpu.VMEM((8, width), F32),
                pltpu.VMEM((width, 256), F32),
                pltpu.VMEM(w_qkv.shape, BF),
                pltpu.VMEM(turned.shape, BF),
                pltpu.SemaphoreType.DMA((2,)),
            ],
        ),
        out_shape=outs,
        compiler_params=pltpu.CompilerParams(vmem_limit_bytes=SCORES_VMEM),
        cost_estimate=cost(24 * 10**9, 34 * 2**20),
        name="scores_backward",
    )(order, joined, weights, natural, proj, att_grad, val_grad, grads, places, w_qkv, gain, turned)


def gray(place):
    return place ^ (place >> 1)


def row_orders():
    place = jnp.arange(128, dtype=jnp.int32)
    core = lax.axis_index("core") ^ (place >> 6)

    def block(y, zh, x, zl):
        return (((y * 2 + zh) * 4 + x) * 2 + core) * 2 + zl

    direct = block(*digits(place & 63, 4, 2, 4, 2))
    one, two, y, zh, zl = digits(place & 63, 2, 2, 4, 2, 2)
    mask = jnp.where(core == 0, one + 2 * two, 2 * one + two)
    x = gray(gray(lax.axis_index("x")) ^ mask)
    return jnp.stack([direct, block(y, zh, x, zl)]).astype(jnp.int32)


def neighbours(step):
    pairs = []
    for place in range(4):
        for core in range(2):
            mask = 1 if step == core else 2
            pairs.append((place * 2 + core, gray(gray(place) ^ mask) * 2 + core))
    return pairs


def after_kernel(*refs):
    del refs


def after(other, *held, space=pltpu.HBM, room=SCORES_VMEM):
    anywhere = pl.BlockSpec(memory_space=space)
    return pl.pallas_call(
        after_kernel,
        in_specs=[anywhere] * (len(held) + 1),
        out_specs=[anywhere] * len(held),
        out_shape=[jax.ShapeDtypeStruct(h.shape, h.dtype) for h in held],
        input_output_aliases={i + 1: i for i in range(len(held))},
        compiler_params=pltpu.CompilerParams(vmem_limit_bytes=room),
        name="after",
    )(other, *held)


def add(a, b):
    return (a.astype(F32) + b.astype(F32)).astype(BF)


def halves_sum(held, got):
    half = held.shape[0] // 2
    return add(held[:half], got[:half]), add(held[half:], got[half:])


def sum_along_x(keep, send):
    keep, send = halves_sum(keep, lax.ppermute(send, "core", [(0, 1), (1, 0)]))
    keep, send = halves_sum(keep, lax.ppermute(send, ("x", "core"), neighbours(0)))
    return add(keep, lax.ppermute(send, ("x", "core"), neighbours(1)))


def join_cores(keep, send):
    return add(keep, lax.ppermute(send, "core", [(0, 1), (1, 0)]))


def to_owners(joined, axes, count):
    rows, columns = joined.shape
    return lax.all_to_all(joined.reshape(count, rows // count, columns), axes, 0, 0, tiled=True)


def on_device(layer_input, out_grad, slot_frame, ln_gain, ln_bias, w_qkv, w_out, time_bias):
    width = layer_input.shape[-1]
    frames = slot_frame.shape[1]
    rows_in = lax.all_to_all(split_patches(layer_input), SEQ, 0, 0, tiled=True)
    split_grad, table = prepare(out_grad, time_bias, frames)
    rows_grad = lax.all_to_all(split_grad, SEQ, 0, 0, tiled=True)
    orders = row_orders()
    gain, bias = ln_gain.reshape(1, width), ln_bias.reshape(1, width)
    places, turned, proj, weights, natural, att = forward(rows_in, gain, bias, w_qkv, table)
    grads, att_grad, val_grad, keep, send = values_backward(
        orders, rows_grad, slot_frame, w_out, weights, att, turned
    )
    joined = join_cores(keep, send)
    parts = to_owners(joined, CHIPS, 64)
    out_rows, keep, send = scores_backward(
        orders, joined, weights, natural, proj, att_grad, val_grad, grads, places, w_qkv, gain, turned
    )
    out_rows, keep, send = after(parts, out_rows, keep, send)
    out_parts = lax.all_to_all(out_rows, SEQ, 0, 0, tiled=True)
    held = sum_along_x(keep, send)
    in_grad = merge_patches(out_parts)
    (held,) = after(out_parts, held, space=pl.ANY, room=2**20)
    first_sums = jnp.sum(parts.astype(F32), axis=0)
    second_sums = jnp.sum(to_owners(held, PLANE, 16).astype(F32), axis=0)
    tokens = 128 * SPAN * frames
    scale = float(tokens) ** (-0.5)
    first_sums = first_sums * scale
    second_sums = second_sums * scale
    qkv_grad = jnp.concatenate([second_sums[:, : 2 * width], first_sums[:, :width]], axis=1)
    tail = second_sums[:, 2 * width :]
    return (in_grad, qkv_grad, first_sums[:, width:], tail[:, 0], tail[:, 1])


def solution(mesh):
    inner = Mesh(mesh.devices.reshape(4, 2, 4, 2, 2), ("y", "zh", "x", "core", "zl"))
    every = ("y", "zh", "x", "core", "zl")
    return jax.shard_map(
        on_device,
        mesh=inner,
        in_specs=(P("zl", SEQ, None, None), P("zl", SEQ, None, None), P("zl", None), P(), P(), P(), P(), P()),
        out_specs=(P("zl", SEQ, None, None), P(every, None), P(every, None), P(every), P(every)),
        check_vma=False,
    )
```

```python
import functools

import jax
import jax.numpy as jnp
from jax import lax
from jax.experimental import pallas as pl
from jax.experimental.pallas import tpu as pltpu
from jax.sharding import Mesh, PartitionSpec as P

BF = jnp.bfloat16
F32 = jnp.float32
VMEM_BYTES = 36 * 1024 * 1024
SCORES_VMEM = 60 * 1024 * 1024
SPAN = 4
GROUP = 16
PAIR = 128
SEQ = ("y", "zh", "x", "core")
CHIPS = ("y", "zh", "x", "zl")
PLANE = ("y", "zh", "zl")

NT = (((1,), (1,)), ((), ()))
TN = (((0,), (0,)), ((), ()))


def mm(a, b, dims=(((1,), (0,)), ((), ()))):
    return lax.dot_general(a, b, dims, preferred_element_type=F32)


def params(*semantics):
    return pltpu.CompilerParams(vmem_limit_bytes=VMEM_BYTES)


def cost(flops, moved, transcendentals=0):
    return pl.CostEstimate(flops=flops, bytes_accessed=moved, transcendentals=transcendentals)


def full(shape):
    return pl.BlockSpec(shape, lambda *ids: (0,) * len(shape), pipeline_mode=pl.Buffered(1))


def digits(index, *sizes):
    out = []
    for size in reversed(sizes):
        out.append(lax.rem(index, size))
        index = lax.div(index, size)
    return out[::-1]


def one_hot_rows(targets, shape, axis):
    return (targets == lax.broadcasted_iota(jnp.int32, shape, axis)).astype(F32).astype(BF)


def frame_major_from(shape):
    row = lax.broadcasted_iota(jnp.int32, shape, 0)
    block, place, frame = digits(row, GROUP, SPAN, SPAN)
    return one_hot_rows((frame * GROUP + block) * SPAN + place, shape, 1)


def frame_major_to(shape):
    col = lax.broadcasted_iota(jnp.int32, shape, 1)
    block, place, frame = digits(col, GROUP, SPAN, SPAN)
    return one_hot_rows((frame * GROUP + block) * SPAN + place, shape, 0)


def place_major_from(shape):
    col = lax.broadcasted_iota(jnp.int32, shape, 1)
    block, place, frame = digits(col, GROUP, SPAN, SPAN)
    return one_hot_rows((place * GROUP + block) * SPAN + frame, shape, 0)


def place_major_to(shape):
    row = lax.broadcasted_iota(jnp.int32, shape, 0)
    block, place, frame = digits(row, GROUP, SPAN, SPAN)
    return one_hot_rows((place * GROUP + block) * SPAN + frame, shape, 1)


SQUARE = (GROUP * SPAN * SPAN, GROUP * SPAN * SPAN)


def split_kernel(rows_ref, out_ref):
    spread = rows_ref[0].reshape(SQUARE[0], rows_ref.shape[-1])
    moved = mm(frame_major_from(SQUARE), spread).astype(BF)
    out_ref[...] = moved.reshape(out_ref.shape)


def split_patches(rows):
    _, span, patches, width = rows.shape
    blocks = patches // span
    return pl.pallas_call(
        split_kernel,
        grid=(blocks // GROUP,),
        in_specs=[pl.BlockSpec((1, span, GROUP * span, width), lambda c: (0, 0, c, 0))],
        out_specs=pl.BlockSpec((GROUP, span * span, width), lambda c: (c, 0, 0)),
        out_shape=jax.ShapeDtypeStruct((blocks, span * span, width), BF),
        compiler_params=params(),
        cost_estimate=cost(2 * 256 * rows.size, 4 * rows.size),
        name="split_patches",
    )(rows)


def merge_kernel(rows_ref, out_ref):
    moved = mm(frame_major_to(SQUARE), rows_ref[...].reshape(SQUARE[0], rows_ref.shape[-1]))
    out_ref[0] = moved.astype(BF).reshape(out_ref.shape[1:])


def merge_patches(rows):
    blocks, rows_each, width = rows.shape
    return pl.pallas_call(
        merge_kernel,
        grid=(blocks // GROUP,),
        in_specs=[pl.BlockSpec((GROUP, rows_each, width), lambda c: (c, 0, 0))],
        out_specs=pl.BlockSpec((1, SPAN, GROUP * SPAN, width), lambda c: (0, 0, c, 0)),
        out_shape=jax.ShapeDtypeStruct((1, SPAN, blocks * SPAN, width), BF),
        compiler_params=params(),
        cost_estimate=cost(2 * 256 * rows.size, 4 * rows.size),
        name="merge_patches",
    )(rows)


def prepare_kernel(rows_ref, bias_ref, out_ref, table_ref):
    split_kernel(rows_ref, out_ref)
    heads, frames, _ = table_ref.shape
    for h in range(heads):
        wide = jnp.broadcast_to(bias_ref[h], (frames, 2 * frames))
        table_ref[h] = pltpu.roll(wide, frames + 1, 1, stride=1, stride_axis=0)[:, :frames]


def prepare(rows, time_bias, frames):
    _, span, patches, width = rows.shape
    blocks = patches // span
    steps = blocks // GROUP
    heads = time_bias.shape[0]
    turned = jnp.pad(time_bias[:, ::-1], ((0, 0), (0, 1))).reshape(heads, 1, 2 * frames)
    return pl.pallas_call(
        prepare_kernel,
        grid=(steps,),
        in_specs=[
            pl.BlockSpec((1, span, GROUP * span, width), lambda c: (0, 0, c, 0)),
            pl.BlockSpec((heads // steps, 1, 2 * frames), lambda c: (c, 0, 0)),
        ],
        out_specs=[
            pl.BlockSpec((GROUP, span * span, width), lambda c: (c, 0, 0)),
            pl.BlockSpec((heads // steps, frames, frames), lambda c: (c, 0, 0)),
        ],
        out_shape=[
            jax.ShapeDtypeStruct((blocks, span * span, width), BF),
            jax.ShapeDtypeStruct((heads, frames, frames), F32),
        ],
        compiler_params=params(),
        cost_estimate=cost(2 * 256 * rows.size, 4 * rows.size + 4 * 2**20),
        name="prepare",
    )(rows, turned)


def gather_places(rows_ref, out_ref):
    blocks, _, width = rows_ref.shape
    order = place_major_from(SQUARE)
    run = GROUP * SPAN
    for c in range(blocks // GROUP):
        chunk = rows_ref[c * GROUP : (c + 1) * GROUP].reshape(SQUARE[0], width)
        moved = mm(order, chunk).astype(BF)
        for p in range(SPAN):
            out_ref[p, c * run : (c + 1) * run, :] = moved[p * run : (p + 1) * run, :]


def norm_parts(values):
    mean = jnp.mean(values, axis=-1, keepdims=True)
    centred = values - mean
    inv_std = lax.rsqrt(jnp.mean(centred * centred, axis=-1, keepdims=True) + 1e-05)
    return centred * inv_std, inv_std


def halves(frames):
    return lax.broadcasted_iota(jnp.int32, (frames, PAIR), 1) < PAIR // 2


def forward_kernel(
    rows_ref, gain_ref, bias_ref, w_ref, table_ref,
    places_ref, turned_ref, proj_ref, weights_ref, natural_ref, att_ref, places,
):
    step = pl.program_id(0)

    @pl.when(step == 0)
    def _():
        gather_places(rows_ref, places)

    rows = places[step]
    places_ref[0] = rows
    normed, _ = norm_parts(rows.astype(F32))
    hidden = (normed * gain_ref[...] + bias_ref[...]).astype(BF)
    turned_ref[...] = hidden.T
    width = hidden.shape[1]
    factor = 0.125
    proj_ref[0, :, :width] = (mm(hidden, w_ref[:, :width]) * factor).astype(BF)
    proj_ref[0, :, width : 2 * width] = mm(hidden, w_ref[:, width : 2 * width]).astype(BF)
    proj_ref[0, :, 2 * width :] = mm(hidden, w_ref[:, 2 * width :]).astype(BF)
    frames = rows.shape[0]
    first = halves(frames)
    for i in range(width // PAIR):
        lanes = slice(i * PAIR, (i + 1) * PAIR)
        queries = proj_ref[0, :, lanes]
        keys = proj_ref[0, :, width + i * PAIR : width + (i + 1) * PAIR]
        vals = proj_ref[0, :, 2 * width + i * PAIR : 2 * width + (i + 1) * PAIR]
        parts = []
        for h in range(2):
            mine = jnp.where(first if h == 0 else ~first, keys, jnp.zeros_like(keys))
            scores = mm(mine, queries, NT) + table_ref[2 * i + h]
            top = jnp.max(scores, axis=0, keepdims=True)
            raised = jnp.exp(scores - top)
            total = jnp.sum(raised, axis=0, keepdims=True)
            short = (raised * (1.0 / total)).astype(BF)
            weights_ref[0, 2 * i + h] = short
            natural = short.T
            natural_ref[0, 2 * i + h] = natural
            parts.append(mm(natural, vals))
        att_ref[0, :, lanes] = jnp.where(first, parts[0], parts[1]).astype(BF)


def forward(rows, gain, bias, w_qkv, table):
    blocks, _, width = rows.shape
    frames = blocks * SPAN
    heads = table.shape[0]
    per = lambda *tail: pl.BlockSpec((1,) + tail, lambda p: (p,) + (0,) * len(tail))
    return pl.pallas_call(
        forward_kernel,
        grid=(SPAN,),
        in_specs=[full(rows.shape), full((1, width)), full((1, width)), full(w_qkv.shape),
                  full(table.shape)],
        out_specs=[
            per(frames, width),
            pl.BlockSpec((width, frames), lambda p: (0, p)),
            per(frames, 3 * width),
            per(heads, frames, frames),
            per(heads, frames, frames),
            per(frames, width),
        ],
        out_shape=[
            jax.ShapeDtypeStruct((SPAN, frames, width), BF),
            jax.ShapeDtypeStruct((width, SPAN * frames), BF),
            jax.ShapeDtypeStruct((SPAN, frames, 3 * width), BF),
            jax.ShapeDtypeStruct((SPAN, heads, frames, frames), BF),
            jax.ShapeDtypeStruct((SPAN, heads, frames, frames), BF),
            jax.ShapeDtypeStruct((SPAN, frames, width), BF),
        ],
        scratch_shapes=[pltpu.VMEM((SPAN, frames, width), BF)],
        compiler_params=params(),
        cost_estimate=cost(16 * 10**9, 34 * 2**20, 2**22),
        name="forward",
    )(rows, gain, bias, w_qkv, table)


def place_rows(terms, order_ref, line, keep_ref, send_ref, cols):
    count = order_ref.shape[1]
    half = count // 2
    for i in range(0, count, 2):
        pair = []
        for j in (i, i + 1):
            start = pl.multiple_of(order_ref[line, j] * 8, 8)
            pair.append(terms[pl.ds(start, 8), :])
        rows = jnp.concatenate(pair, axis=0).astype(BF)
        target, at = (keep_ref, i) if i < half else (send_ref, i - half)
        target[at * 8 : at * 8 + 16, cols] = rows


def values_kernel(
    order_ref, rows_ref, slot_ref, w_ref, weights_ref, att_ref, turned_ref,
    grad_ref, att_grad_ref, val_grad_ref, keep_ref, send_ref, places, turned_grad, val_grads, terms,
):
    step = pl.program_id(0)

    @pl.when(step == 0)
    def _():
        gather_places(rows_ref, places)

    frames, width = places.shape[1:]
    natural = one_hot_rows(slot_ref[...], (frames, frames), 0)
    grads = mm(natural, places[step]).astype(BF)
    grad_ref[0] = grads
    here = pl.ds(pl.multiple_of(step * frames, frames), frames)
    turned_grad[:, here] = grads.T
    att_grad_ref[0] = mm(grads, w_ref[...], NT).astype(BF)
    first = halves(frames)
    for i in range(width // PAIR):
        lanes = slice(i * PAIR, (i + 1) * PAIR)
        att_grad = att_grad_ref[0, :, lanes]
        parts = [mm(weights_ref[0, 2 * i + h], att_grad) for h in range(2)]
        merged = jnp.where(first, parts[0], parts[1]).astype(BF)
        val_grad_ref[0, :, lanes] = merged
        val_grads[here, lanes] = merged

    @pl.when(step == pl.num_programs(0) - 1)
    def _():
        chunk = terms.shape[1]
        for c in range(width // chunk):
            cols = slice(c * chunk, (c + 1) * chunk)
            after = slice(width + c * chunk, width + (c + 1) * chunk)
            terms[...] = mm(turned_ref[...], val_grads[:, cols])
            place_rows(terms, order_ref, 0, keep_ref, send_ref, cols)
            terms[...] = mm(turned_grad[...], att_ref[:, :, cols].reshape(SPAN * frames, chunk))
            place_rows(terms, order_ref, 0, keep_ref, send_ref, after)


def values_backward(order, rows, slot_frame, w_out, weights, att, turned):
    blocks, _, width = rows.shape
    frames = blocks * SPAN
    heads = weights.shape[1]
    tokens = SPAN * frames
    per = lambda *tail: pl.BlockSpec((1,) + tail, lambda p, _: (p,) + (0,) * len(tail))
    rows_each = jax.ShapeDtypeStruct((SPAN, frames, width), BF)
    half = jax.ShapeDtypeStruct((width // 2, 2 * width), BF)
    return pl.pallas_call(
        values_kernel,
        grid_spec=pltpu.PrefetchScalarGridSpec(
            num_scalar_prefetch=1,
            grid=(SPAN,),
            in_specs=[full(rows.shape), full(slot_frame.shape), full(w_out.shape), per(heads, frames, frames),
                      full(att.shape), full(turned.shape)],
            out_specs=[per(frames, width), per(frames, width), per(frames, width), full(half.shape), full(half.shape)],
            scratch_shapes=[
                pltpu.VMEM((SPAN, frames, width), BF),
                pltpu.VMEM((width, tokens), BF),
                pltpu.VMEM((tokens, width), BF),
                pltpu.VMEM((width, 256), F32),
            ],
        ),
        out_shape=[rows_each, rows_each, rows_each, half, half],
        compiler_params=params(),
        cost_estimate=cost(12 * 10**9, 28 * 2**20),
        name="values_backward",
    )(order, rows, slot_frame, w_out, weights, att, turned)


def scores_kernel(
    order_ref, joined_ref, weights_ref, natural_ref, proj_ref, att_grad_ref, val_grad_ref, grad_ref, places_ref, w_far, gain_ref,
    turned_far, out_far, keep_far, send_far,
    results, pairs, sums, terms, w_ref, turned_ref, out_ref, keep_ref, send_ref, arrived, left,
):
    step = pl.program_id(0)
    copies = [
        pltpu.make_async_copy(w_far, w_ref, arrived.at[0]),
        pltpu.make_async_copy(turned_far, turned_ref, arrived.at[1]),
    ]

    @pl.when(step == 0)
    def _():
        for copy in copies:
            copy.start()

    frames, width = grad_ref.shape[1:]
    first = halves(frames)
    factor = 0.125
    here = pl.ds(pl.multiple_of(step * frames, frames), frames)
    for i in range(width // PAIR):
        lanes = slice(i * PAIR, (i + 1) * PAIR)
        key_lanes = slice(width + i * PAIR, width + (i + 1) * PAIR)
        queries = proj_ref[0, :, lanes]
        keys = proj_ref[0, :, key_lanes]
        vals = proj_ref[0, :, 2 * width + i * PAIR : 2 * width + (i + 1) * PAIR]
        att_grad = att_grad_ref[0, :, lanes]
        key_parts, query_parts = [], []
        for h in range(2):
            mine = jnp.where(first if h == 0 else ~first, vals, jnp.zeros_like(vals))
            weight_grad = mm(mine, att_grad, NT)
            weights = weights_ref[0, 2 * i + h].astype(F32)
            shared = jnp.sum(weight_grad * weights, axis=0, keepdims=True)
            score_grad = (weights * (weight_grad - shared)).astype(BF)
            key_parts.append(mm(score_grad, queries))
            weight_grad = mm(jnp.where(first if h == 0 else ~first, att_grad, jnp.zeros_like(att_grad)), vals, NT)
            weights = natural_ref[0, 2 * i + h].astype(F32)
            shared = jnp.sum(weight_grad * weights, axis=1, keepdims=True)
            query_parts.append(mm((weights * (weight_grad - shared)).astype(BF), keys))
        pairs[here, lanes] = (jnp.where(first, query_parts[0], query_parts[1]) * factor).astype(BF)
        pairs[here, key_lanes] = jnp.where(first, key_parts[0], key_parts[1]).astype(BF)

    @pl.when(step == 0)
    def _():
        for copy in copies:
            copy.wait()

    hidden_grad = mm(pairs[here, :], w_ref[:, : 2 * width], NT) + mm(val_grad_ref[0], w_ref[:, 2 * width :], NT)
    normed, inv_std = norm_parts(places_ref[0].astype(F32))
    scaled = hidden_grad * gain_ref[...]
    norm_grad = inv_std * (
        scaled
        - jnp.mean(scaled, axis=-1, keepdims=True)
        - normed * jnp.mean(scaled * normed, axis=-1, keepdims=True)
    )
    results[step] = (grad_ref[0].astype(F32) + norm_grad).astype(BF)
    gain_term = jnp.sum(hidden_grad * normed, axis=0, keepdims=True)
    bias_term = jnp.sum(hidden_grad, axis=0, keepdims=True)

    @pl.when(step == 0)
    def _():
        sums[...] = jnp.zeros_like(sums)

    sums[0:1, :] += gain_term
    sums[1:2, :] += bias_term

    @pl.when(step == pl.num_programs(0) - 1)
    def _():
        leaving = []

        def leave(near, far, where, value=None):
            if value is not None:
                near[where] = value
            leaving.append(pltpu.make_async_copy(near.at[where], far.at[where], left.at[len(leaving)]))
            leaving[-1].start()

        order = place_major_to(SQUARE)
        run = GROUP * SPAN
        for c in range(frames // run):
            chunk = results[:, c * run : (c + 1) * run, :].reshape(SQUARE[0], width)
            moved = mm(order, chunk).astype(BF)
            leave(out_ref, out_far, slice(c * GROUP, (c + 1) * GROUP), moved.reshape(GROUP, SPAN * SPAN, width))
        chunk = terms.shape[1]
        for at in range(0, 2 * width, chunk):
            cols = slice(at, at + chunk)
            terms[...] = mm(turned_ref[...], pairs[:, cols])
            place_rows(terms, order_ref, 1, keep_ref, send_ref, cols)
            leave(keep_ref, keep_far, (slice(None), cols))
            leave(send_ref, send_far, (slice(None), cols))
        cols = slice(2 * width, 2 * width + PAIR)
        terms[:, :PAIR] = jnp.concatenate([sums[...]] * (PAIR // sums.shape[0]), axis=0).T
        place_rows(terms.at[:, :PAIR], order_ref, 1, keep_ref, send_ref, cols)
        leave(keep_ref, keep_far, (slice(None), cols))
        leave(send_ref, send_far, (slice(None), cols))
        for copy in leaving:
            copy.wait()


def scores_backward(order, joined, weights, natural, proj, att_grad, val_grad, grads, places, w_qkv, gain, turned):
    _, frames, width = grads.shape
    heads = weights.shape[1]
    blocks = frames // SPAN
    tokens = SPAN * frames
    per = lambda *tail: pl.BlockSpec((1,) + tail, lambda p, _: (p,) + (0,) * len(tail))
    half = jax.ShapeDtypeStruct((width // 2, 2 * width + PAIR), BF)
    outs = [jax.ShapeDtypeStruct((blocks, SPAN * SPAN, width), BF), half, half]
    return pl.pallas_call(
        scores_kernel,
        grid_spec=pltpu.PrefetchScalarGridSpec(
            num_scalar_prefetch=1,
            grid=(SPAN,),
            in_specs=[pl.BlockSpec(memory_space=pl.ANY), per(heads, frames, frames), per(heads, frames, frames),
                      per(frames, 3 * width),
                      per(frames, width), per(frames, width), per(frames, width), per(frames, width),
                      pl.BlockSpec(memory_space=pl.ANY), full((1, width)), pl.BlockSpec(memory_space=pl.ANY)],
            out_specs=[pl.BlockSpec(memory_space=pl.ANY)] * len(outs),
            scratch_shapes=[
                pltpu.VMEM((SPAN, frames, width), BF),
                pltpu.VMEM((tokens, 2 * width), BF),
                pltpu.VMEM((8, width), F32),
                pltpu.VMEM((width, 256), F32),
                pltpu.VMEM(w_qkv.shape, BF),
                pltpu.VMEM(turned.shape, BF),
                *[pltpu.VMEM(o.shape, BF) for o in outs],
                pltpu.SemaphoreType.DMA((2,)),
                pltpu.SemaphoreType.DMA((32,)),
            ],
        ),
        out_shape=outs,
        compiler_params=pltpu.CompilerParams(vmem_limit_bytes=SCORES_VMEM),
        cost_estimate=cost(24 * 10**9, 34 * 2**20),
        name="scores_backward",
    )(order, joined, weights, natural, proj, att_grad, val_grad, grads, places, w_qkv, gain, turned)


def gray(place):
    return place ^ (place >> 1)


def row_orders():
    place = jnp.arange(128, dtype=jnp.int32)
    core = lax.axis_index("core") ^ (place >> 6)

    def block(y, zh, x, zl):
        return (((y * 2 + zh) * 4 + x) * 2 + core) * 2 + zl

    direct = block(*digits(place & 63, 4, 2, 4, 2))
    one, two, y, zh, zl = digits(place & 63, 2, 2, 4, 2, 2)
    mask = jnp.where(core == 0, one + 2 * two, 2 * one + two)
    x = gray(gray(lax.axis_index("x")) ^ mask)
    return jnp.stack([direct, block(y, zh, x, zl)]).astype(jnp.int32)


def neighbours(step):
    pairs = []
    for place in range(4):
        for core in range(2):
            mask = 1 if step == core else 2
            pairs.append((place * 2 + core, gray(gray(place) ^ mask) * 2 + core))
    return pairs


def after_kernel(*refs):
    del refs


def after(other, *held, space=pltpu.HBM, room=SCORES_VMEM):
    anywhere = pl.BlockSpec(memory_space=space)
    return pl.pallas_call(
        after_kernel,
        in_specs=[anywhere] * (len(held) + 1),
        out_specs=[anywhere] * len(held),
        out_shape=[jax.ShapeDtypeStruct(h.shape, h.dtype) for h in held],
        input_output_aliases={i + 1: i for i in range(len(held))},
        compiler_params=pltpu.CompilerParams(vmem_limit_bytes=room),
        name="after",
    )(other, *held)


def add(a, b):
    return (a.astype(F32) + b.astype(F32)).astype(BF)


def halves_sum(held, got):
    half = held.shape[0] // 2
    return add(held[:half], got[:half]), add(held[half:], got[half:])


def sum_along_x(keep, send):
    keep, send = halves_sum(keep, lax.ppermute(send, "core", [(0, 1), (1, 0)]))
    keep, send = halves_sum(keep, lax.ppermute(send, ("x", "core"), neighbours(0)))
    return add(keep, lax.ppermute(send, ("x", "core"), neighbours(1)))


def join_cores(keep, send):
    return add(keep, lax.ppermute(send, "core", [(0, 1), (1, 0)]))


def to_owners(joined, axes, count):
    rows, columns = joined.shape
    return lax.all_to_all(joined.reshape(count, rows // count, columns), axes, 0, 0, tiled=True)


def on_device(layer_input, out_grad, slot_frame, ln_gain, ln_bias, w_qkv, w_out, time_bias):
    width = layer_input.shape[-1]
    frames = slot_frame.shape[1]
    rows_in = lax.all_to_all(split_patches(layer_input), SEQ, 0, 0, tiled=True)
    split_grad, table = prepare(out_grad, time_bias, frames)
    rows_grad = lax.all_to_all(split_grad, SEQ, 0, 0, tiled=True)
    orders = row_orders()
    gain, bias = ln_gain.reshape(1, width), ln_bias.reshape(1, width)
    places, turned, proj, weights, natural, att = forward(rows_in, gain, bias, w_qkv, table)
    grads, att_grad, val_grad, keep, send = values_backward(
        orders, rows_grad, slot_frame, w_out, weights, att, turned
    )
    joined = join_cores(keep, send)
    parts = to_owners(joined, CHIPS, 64)
    out_rows, keep, send = scores_backward(
        orders, joined, weights, natural, proj, att_grad, val_grad, grads, places, w_qkv, gain, turned
    )
    out_rows, keep, send = after(parts, out_rows, keep, send)
    out_parts = lax.all_to_all(out_rows, SEQ, 0, 0, tiled=True)
    held = sum_along_x(keep, send)
    in_grad = merge_patches(out_parts)
    (held,) = after(out_parts, held, space=pl.ANY, room=2**20)
    first_sums = jnp.sum(parts.astype(F32), axis=0)
    second_sums = jnp.sum(to_owners(held, PLANE, 16).astype(F32), axis=0)
    tokens = 128 * SPAN * frames
    scale = float(tokens) ** (-0.5)
    first_sums = first_sums * scale
    second_sums = second_sums * scale
    qkv_grad = jnp.concatenate([second_sums[:, : 2 * width], first_sums[:, :width]], axis=1)
    tail = second_sums[:, 2 * width :]
    return (in_grad, qkv_grad, first_sums[:, width:], tail[:, 0], tail[:, 1])


def solution(mesh):
    inner = Mesh(mesh.devices.reshape(4, 2, 4, 2, 2), ("y", "zh", "x", "core", "zl"))
    every = ("y", "zh", "x", "core", "zl")
    return jax.shard_map(
        on_device,
        mesh=inner,
        in_specs=(P("zl", SEQ, None, None), P("zl", SEQ, None, None), P("zl", None), P(), P(), P(), P(), P()),
        out_specs=(P("zl", SEQ, None, None), P(every, None), P(every, None), P(every), P(every)),
        check_vma=False,
    )
```
